512 devices in a mesh: frame: 64 (over y, x, core), row: 8 (over z).
Axes of the slice: x: 4, y: 8, z: 8, core: 2. Of those that a mesh axis runs over, the one named last changes fastest.
Arguments:
- tokens: bfloat16 [64, 8, 128, 2048], P('frame', 'row'), may hold values from -6 to 6
- cotangent: bfloat16 [64, 8, 128, 2048], P('frame', 'row'), may hold values from -6 to 6
- timestep: int32 [4], replicated, may hold values from 0 to 999
- mod_weight: bfloat16 [256, 4096], P(None, 'frame'), may hold values from -0.375 to 0.375
- proj_weight: bfloat16 [2048, 256], P('frame'), may hold values from -0.125 to 0.125
- step_weight: bfloat16 [2048, 32], P('frame'), may hold values from -0.125 to 0.125
- step_bias: float32 [32], replicated, may hold values from -1 to 1
- rate_space: float32 [32], replicated, may hold values from 0.00029296876 to 0.05
- rate_time: float32 [32], replicated, may hold values from 0.0046875 to 1
- skip_gain: float32 [32], replicated, may hold values from 0.5 to 1.5
Outputs:
- mixed: bfloat16 [64, 8, 128, 2048], P('frame', 'row')
- d_tokens: bfloat16 [64, 8, 128, 2048], P('frame', 'row')
- grad_proj: float32 [2048, 256], P('frame')
- grad_step: float32 [2048, 32], P('frame')
- grad_mod: float32 [256, 4096], P(None, 'frame')
The draws below stay inside these ranges and needn't reach their ends.
All inputs are finite; a program needn't handle non-finite values.
Results may differ from the reference program's by a relative error of at most 0.015.
Values may be sent and summed in bfloat16 or wider, within the bound.
A program may use at most 64 MiB of HBM per device.

```python
import math
import jax
import jax.numpy as jnp
from jax import lax

HEADS = 32
HEAD_DIM = 64
WIDTH = 2048
STATE = 128
EMBED = 256
CLIP_LEN = 16
COLS = 128
ROWS_DEV = 1
LATENT_ROWS = 8
FRAMES = 64
CLIPS = 4
TOKENS = 65536


def touch_ends(drawn, key, smallest, top_value):
    longest = drawn.shape.index(max(drawn.shape))
    spots = []
    for shift in (0, 1):
        where = [jax.random.randint(jax.random.fold_in(key, axis), (), 0, length) for axis, length in enumerate(drawn.shape)]
        where[longest] = (where[longest] + shift) % drawn.shape[longest]
        spots.append(tuple(where))
    return drawn.at[spots[0]].set(smallest).at[spots[1]].set(top_value)


def level_of(key, extent, cuts, low, top_value):
    level = 1.0
    for position, shards_of in cuts:
        heights = jax.random.uniform(jax.random.fold_in(jax.random.fold_in(key, 6), position), (shards_of,), jnp.float32, low / len(cuts), top_value / len(cuts))
        level = level * jnp.repeat(jnp.exp(heights), extent[position] // shards_of).reshape((-1,) + (1,) * (len(extent) - 1 - position))
    return level


def bell_draw(own_key, dims, scale, reach, cuts=(), held_as=jnp.bfloat16):
    result = jax.random.normal(own_key, dims, jnp.float32) * scale
    if len(cuts) > 0:
        result = level_of(own_key, dims, cuts, -0.22, 0.18) * result
    return jnp.clip(result, min=-reach, max=reach).astype(held_as)


def setup_inputs(seed: int = 0) -> dict:
    keys = jax.random.split(jax.random.key(seed), 11)
    return {
        "tokens": bell_draw(keys[0], (FRAMES, LATENT_ROWS, COLS, WIDTH), 1.0, 6.0, ((0, 64), (1, 8))),
        "cotangent": bell_draw(keys[1], (FRAMES, LATENT_ROWS, COLS, WIDTH), 1.0, 6.0, ((0, 64), (1, 8))),
        "timestep": touch_ends(jax.random.randint(keys[2], (CLIPS,), 0, 1000), jax.random.fold_in(keys[2], 1), 0, 999).astype(jnp.int32),
        "mod_weight": bell_draw(keys[3], (EMBED, 2 * WIDTH), EMBED ** -0.5, 0.375, ((1, 64),)),
        "proj_weight": bell_draw(keys[4], (WIDTH, 2 * STATE), WIDTH ** -0.5, 0.125, ((0, 64),)),
        "step_weight": bell_draw(keys[5], (WIDTH, HEADS), WIDTH ** -0.5, 0.125, ((0, 64),)),
        "step_bias": jnp.clip(jax.random.uniform(keys[6], (HEADS,), jnp.float32, -1.0, 1.0), -1.0, 1.0),
        "rate_space": jnp.clip(jnp.exp(jax.random.uniform(keys[7], (HEADS,), jnp.float32, math.log(0.00029296876), math.log(0.05))), 0.00029296876, 0.05),
        "rate_time": jnp.clip(jnp.exp(jax.random.uniform(keys[8], (HEADS,), jnp.float32, math.log(0.0046875), math.log(1.0))), 0.0046875, 1.0),
        "skip_gain": jnp.clip(jax.random.uniform(keys[9], (HEADS,), jnp.float32, 0.5, 1.5), 0.5, 1.5),
    }


norm_eps = 1e-05

def time_embed(timestep, embed_dim):
    half_dim = embed_dim // 2
    frequency = jnp.exp(-math.log(10000.0) * jnp.arange(half_dim, dtype=jnp.float32) / half_dim)
    angles = timestep.astype(jnp.float32)[:, None] * frequency[None, :]
    return jax.nn.silu(jnp.concatenate([jnp.cos(angles), jnp.sin(angles)], axis=1))

def normalize(values):
    return values * lax.rsqrt(lax.optimization_barrier(jnp.mean(values * values, axis=-1, keepdims=True)) + norm_eps)

def block_parts(normed, coeffs, logits, step_bias, decay_rate, need_end):
    seq_count, length, feat_width = normed.shape
    head_count = decay_rate.shape[0]
    inputs = normed.reshape(seq_count, length, head_count, feat_width // head_count)
    state_size = coeffs.shape[-1] // 2
    b_part = coeffs[..., :state_size]
    c_part = coeffs[..., state_size:]
    step_size = jax.nn.softplus(logits.astype(jnp.float32) + step_bias)
    cum_log = jnp.cumsum(-step_size * decay_rate, axis=1)
    scores = jnp.einsum('stn,sun->stu', c_part, b_part, preferred_element_type=jnp.float32) / state_size
    lag_rows = jnp.swapaxes(cum_log, 1, 2)
    causal = jnp.tril(jnp.ones((length, length), dtype=bool))
    differences = lag_rows[:, :, :, None] - lag_rows[:, :, None, :]
    decays = jnp.where(causal, jnp.exp(jnp.where(causal, differences, 0.0)), 0.0)
    spread = jnp.swapaxes(step_size, 1, 2)
    weights = (scores[:, None, :, :] * decays * spread[:, :, None, :]).astype(jnp.bfloat16)
    inner_out = jnp.einsum('shtu,suhp->sthp', weights, inputs, preferred_element_type=jnp.float32)
    inner_out = inner_out.reshape(seq_count, length, feat_width)
    if need_end:
        end_log = cum_log[:, -1:, :]
        lead_decay = jnp.exp(end_log - cum_log) * step_size
        scaled = (inputs.astype(jnp.float32) * lead_decay[..., None]).astype(jnp.bfloat16)
        end_local = jnp.einsum('sthp,stn->shpn', scaled, b_part, preferred_element_type=jnp.float32)
    else:
        end_local = jnp.zeros((seq_count, head_count, feat_width // head_count, state_size), jnp.float32)
    return (inner_out, end_local, cum_log, c_part)

def carry_term(cum_log, c_part, state_in):
    seq_count, length, head_count = cum_log.shape
    state_size = c_part.shape[-1]
    reached = jnp.einsum('stn,shpn->sthp', c_part.astype(jnp.float32), state_in, precision=lax.Precision.HIGHEST)
    return (reached * jnp.exp(cum_log)[..., None] / state_size).reshape(seq_count, length, -1)

def reference(tokens, cotangent, timestep, mod_weight, proj_weight, step_weight, step_bias, rate_space, rate_time, skip_gain):
    site_total = LATENT_ROWS * COLS
    band_len = ROWS_DEV * COLS
    band_count = LATENT_ROWS // ROWS_DEV
    activated = time_embed(timestep, EMBED).astype(jnp.bfloat16)
    modulation = jnp.dot(activated, mod_weight, preferred_element_type=jnp.float32)
    shift_vec = modulation[:, :WIDTH][:, None, :]
    scale_vec = modulation[:, WIDTH:][:, None, :]
    tokens_wide = tokens.reshape(CLIPS, CLIP_LEN * site_total, WIDTH).astype(jnp.float32)
    unit_rows = normalize(tokens_wide)
    normed = (unit_rows * (1.0 + scale_vec) + shift_vec).astype(jnp.bfloat16).reshape(-1, WIDTH)
    projected = jnp.dot(normed, proj_weight, preferred_element_type=jnp.float32).astype(jnp.bfloat16)
    logits = jnp.dot(normed, step_weight, preferred_element_type=jnp.float32).astype(jnp.bfloat16)
    skip_full = jnp.repeat(skip_gain, HEAD_DIM)

    def space_frame(pieces):

        def one_band(state_in, band_in):
            inner_out, end_local, cum_log, c_part = block_parts(band_in[0], band_in[1], band_in[2], step_bias, rate_space, True)
            output = inner_out + carry_term(cum_log, c_part, state_in)
            state_out = jnp.exp(cum_log[:, -1, :])[:, :, None, None] * state_in + end_local
            return (state_out, output)
        banded = tuple((member.reshape(band_count, 1, band_len, member.shape[-1]) for member in pieces))
        initial = jnp.zeros((1, HEADS, HEAD_DIM, STATE), jnp.float32)
        unused, outputs = lax.scan(one_band, initial, banded)
        return outputs.reshape(site_total, WIDTH)

    def time_rows(pieces):
        sequences = tuple((jnp.swapaxes(member, 0, 1) for member in pieces))
        inner_out = block_parts(sequences[0], sequences[1], sequences[2], step_bias, rate_time, False)[0]
        return jnp.swapaxes(inner_out.astype(jnp.bfloat16), 0, 1)

    def core(normed_s, proj_s, logit_s, normed_t, proj_t, logit_t):
        frame_view = tuple((member.reshape(FRAMES, site_total, member.shape[-1]) for member in (normed_s, proj_s, logit_s)))
        space_out = lax.map(jax.checkpoint(space_frame), frame_view).reshape(-1, WIDTH)
        row_view = tuple((member.reshape(FRAMES, LATENT_ROWS, COLS, member.shape[-1]).transpose(1, 0, 2, 3) for member in (normed_t, proj_t, logit_t)))
        time_out = lax.map(jax.checkpoint(time_rows), row_view)
        time_out = time_out.transpose(1, 0, 2, 3).reshape(-1, WIDTH)
        return space_out + time_out.astype(jnp.float32) + skip_full * normed_s.astype(jnp.float32)
    output, core_pull = jax.vjp(core, normed, projected, logits, normed, projected, logits)
    mixed = output.astype(jnp.bfloat16).reshape(tokens.shape)
    grads = core_pull(cotangent.reshape(-1, WIDTH).astype(jnp.float32))
    space_dnorm, space_dproj, space_dlogit, time_dnorm, time_dproj, time_dlogit = grads
    time_back = (time_dnorm.astype(jnp.float32) + jnp.dot(time_dproj, proj_weight.T, preferred_element_type=jnp.float32) + jnp.dot(time_dlogit, step_weight.T, preferred_element_type=jnp.float32)).astype(jnp.bfloat16)
    pre_grad = space_dnorm.astype(jnp.float32) + jnp.dot(space_dproj, proj_weight.T, preferred_element_type=jnp.float32) + jnp.dot(space_dlogit, step_weight.T, preferred_element_type=jnp.float32) + time_back.astype(jnp.float32)
    factor = TOKENS ** (-0.5)
    grad_proj = (jnp.dot(normed.T, space_dproj, preferred_element_type=jnp.float32) + jnp.dot(normed.T, time_dproj, preferred_element_type=jnp.float32)) * factor
    grad_step = (jnp.dot(normed.T, space_dlogit, preferred_element_type=jnp.float32) + jnp.dot(normed.T, time_dlogit, preferred_element_type=jnp.float32)) * factor
    pre_clip = pre_grad.reshape(CLIPS, -1, WIDTH)
    shift_grad = lax.optimization_barrier(jnp.sum(pre_clip, axis=1))
    scale_grad = lax.optimization_barrier(jnp.sum(pre_clip * unit_rows, axis=1))
    mod_grad = jnp.concatenate([shift_grad, scale_grad], axis=1)
    grad_mod = jnp.dot(activated.astype(jnp.float32).T, mod_grad, precision=lax.Precision.HIGHEST) * factor
    unused, norm_pull = jax.vjp(normalize, tokens_wide)
    tokens_grad, = norm_pull(pre_clip * (1.0 + scale_vec))
    d_tokens = tokens_grad.astype(jnp.bfloat16).reshape(tokens.shape)
    return (mixed, d_tokens, grad_proj, grad_step, grad_mod)
```

```python
import functools
import math

import jax
import jax.numpy as jnp
from jax import lax
from jax.experimental import pallas as pl
from jax.experimental.pallas import tpu as pltpu
from jax.sharding import PartitionSpec as P

norm_eps = 1e-05
MESH = pl.DeviceIdType.MESH
ANY = pl.BlockSpec(memory_space=pl.ANY)
VMEM = pl.BlockSpec(memory_space=pltpu.VMEM)
SMEM = pl.BlockSpec(memory_space=pltpu.SMEM)
CHAIN_CHUNKS = 8


def at(frame=None, row=None):
    place = {}
    if frame is not None:
        place["frame"] = frame
    if row is not None:
        place["row"] = row
    return place


def tell(sem, **place):
    pl.semaphore_signal(sem, inc=1, device_id=at(**place), device_id_type=MESH)


def push(src, dst, send_sem, recv_sem, **place):
    return pltpu.make_async_remote_copy(
        src_ref=src,
        dst_ref=dst,
        send_sem=send_sem,
        recv_sem=recv_sem,
        device_id=at(**place),
        device_id_type=MESH,
    )


def each(start, stop, body):
    def step(k, carry):
        body(k)
        return carry

    lax.fori_loop(start, stop, step, 0)


def gather_kernel(src, out, send1, recv1, send2, recv2, local_sem):
    frame = lax.axis_index("frame")
    chips = lax.axis_size("frame") // 2
    chip, core = frame // 2, frame % 2
    sibling = chip * 2 + (1 - core)
    barrier = pltpu.get_barrier_semaphore()
    each(1, chips, lambda k: tell(barrier, frame=(chip + k) % chips * 2 + core))
    tell(barrier, frame=sibling)
    own = pltpu.make_async_copy(src, out.at[frame], local_sem)
    own.start()
    pl.semaphore_wait(barrier, chips)

    def direct(k):
        peer = (chip + k) % chips * 2 + core
        return push(src, out.at[frame], send1.at[k], recv1.at[k], frame=peer)

    def relay(k):
        origin = (chip + chips - k) % chips * 2 + core
        return push(out.at[origin], out.at[origin], send2.at[k], recv2.at[k], frame=sibling)

    def first(k):
        return push(src, out.at[frame], send2.at[k], recv2.at[k], frame=sibling)

    first(0).start()
    each(1, chips, lambda k: direct(k).start())

    def pass_on(k):
        origin = (chip + chips - k) % chips * 2 + core
        push(src, out.at[origin], send1.at[k], recv1.at[k], frame=sibling).wait_recv()
        relay(k).start()

    each(1, chips, pass_on)

    def finish(k):
        origin = (chip + chips - k) % chips * 2 + (1 - core)
        push(src, out.at[origin], send2.at[k], recv2.at[k], frame=sibling).wait_recv()

    each(0, chips, finish)
    first(0).wait_send()
    each(1, chips, lambda k: direct(k).wait_send())
    each(1, chips, lambda k: relay(k).wait_send())
    own.wait()


def gather(chunk):
    count = lax.axis_size("frame")
    return pl.pallas_call(
        gather_kernel,
        out_shape=jax.ShapeDtypeStruct((count, *chunk.shape), chunk.dtype),
        in_specs=[VMEM],
        out_specs=VMEM,
        scratch_shapes=[
            pltpu.SemaphoreType.DMA((count // 2,)),
            pltpu.SemaphoreType.DMA((count // 2,)),
            pltpu.SemaphoreType.DMA((count // 2,)),
            pltpu.SemaphoreType.DMA((count // 2,)),
            pltpu.SemaphoreType.DMA,
        ],
        compiler_params=pltpu.CompilerParams(collective_id=0, has_side_effects=True),
        name="gather",
    )(chunk)


def plane_copies(frame, count, pairs, send, recv):
    def out_piece(i, k):
        peer = (frame + k) % count
        src, dst = pairs[i]
        return push(src.at[peer], dst.at[frame], send.at[i, k], recv.at[i, k], frame=peer)

    def in_piece(i, k):
        origin = (frame + count - k) % count
        src, dst = pairs[i]
        return push(src.at[origin], dst.at[origin], send.at[i, k], recv.at[i, k], frame=origin)

    return out_piece, in_piece


def plane_start(frame, count, pairs, send, recv, own_sem):
    out_piece, unused = plane_copies(frame, count, pairs, send, recv)
    for i, (src, dst) in enumerate(pairs):
        pltpu.make_async_copy(src.at[frame], dst.at[frame], own_sem.at[i]).start()

    def begin(k):
        for i in range(len(pairs)):
            out_piece(i, k).start()

    each(1, count, begin)


def plane_wait(frame, count, pairs, send, recv, own_sem):
    out_piece, in_piece = plane_copies(frame, count, pairs, send, recv)

    def end(k):
        for i in range(len(pairs)):
            in_piece(i, k).wait_recv()
            out_piece(i, k).wait_send()

    each(1, count, end)
    for i, (src, dst) in enumerate(pairs):
        pltpu.make_async_copy(src.at[frame], dst.at[frame], own_sem.at[i]).wait()


def exchange_chain_kernel(
    xs, gs, end_local, own_grad, decay, rx, rg, state_in, later, fwd_out, bwd_out, send, recv, own_sem,
    fwd_send, fwd_recv, bwd_send, bwd_recv,
):
    frame, row = lax.axis_index("frame"), lax.axis_index("row")
    count, bands = lax.axis_size("frame"), lax.axis_size("row")
    height = end_local.shape[0] // CHAIN_CHUNKS
    heads = decay.shape[0]
    per_head = end_local.shape[0] // heads
    barrier = pltpu.get_barrier_semaphore()
    each(1, count, lambda k: tell(barrier, frame=(frame + k) % count))

    @pl.when(row > 0)
    def _():
        tell(barrier, row=row - 1)

    @pl.when(row < bands - 1)
    def _():
        tell(barrier, row=row + 1)

    neighbours = jnp.where(row > 0, 1, 0) + jnp.where(row < bands - 1, 1, 0)
    pl.semaphore_wait(barrier, count - 1 + neighbours)

    def rows_of(c):
        return pl.ds(c * height, height)

    def fwd(c):
        where = rows_of(c)
        return push(fwd_out.at[where], state_in.at[where], fwd_send.at[c], fwd_recv.at[c], row=row + 1)

    def bwd(c):
        where = rows_of(c)
        return push(bwd_out.at[where], later.at[where], bwd_send.at[c], bwd_recv.at[c], row=row - 1)

    def fwd_in(c):
        where = rows_of(c)
        return push(fwd_out.at[where], state_in.at[where], fwd_send.at[c], fwd_recv.at[c], row=row - 1)

    def bwd_in(c):
        where = rows_of(c)
        return push(bwd_out.at[where], later.at[where], bwd_send.at[c], bwd_recv.at[c], row=row + 1)

    def join(c, before, own, result):
        for j in range(height // per_head):
            where = pl.ds(c * height + j * per_head, per_head)
            factor = decay[c * (height // per_head) + j]
            result[where, :] = (
                before[where, :].astype(jnp.float32) * factor + own[where, :]
            ).astype(result.dtype)

    @pl.when(row == 0)
    def _():
        state_in[...] = jnp.zeros_like(state_in)
        for c in range(CHAIN_CHUNKS):
            fwd_out[rows_of(c), :] = end_local[rows_of(c), :].astype(fwd_out.dtype)
            fwd(c).start()

    @pl.when(row == bands - 1)
    def _():
        later[...] = jnp.zeros_like(later)
        for c in range(CHAIN_CHUNKS):
            bwd_out[rows_of(c), :] = own_grad[rows_of(c), :].astype(bwd_out.dtype)
            bwd(c).start()

    plane_start(frame, count, [(xs, rx), (gs, rg)], send, recv, own_sem)
    for c in range(CHAIN_CHUNKS):

        @pl.when(row > 0)
        def _():
            fwd_in(c).wait_recv()

            @pl.when(row < bands - 1)
            def _():
                join(c, state_in, end_local, fwd_out)
                fwd(c).start()

        @pl.when(row < bands - 1)
        def _():
            bwd_in(c).wait_recv()

            @pl.when(row > 0)
            def _():
                join(c, later, own_grad, bwd_out)
                bwd(c).start()

    plane_wait(frame, count, [(xs, rx), (gs, rg)], send, recv, own_sem)

    @pl.when(row < bands - 1)
    def _():
        for c in range(CHAIN_CHUNKS):
            fwd(c).wait_send()

    @pl.when(row > 0)
    def _():
        for c in range(CHAIN_CHUNKS):
            bwd(c).wait_send()


def exchange_chain(xs, gs, end_local, own_grad, decay):
    count = lax.axis_size("frame")
    state = jax.ShapeDtypeStruct(end_local.shape, jnp.bfloat16)
    return pl.pallas_call(
        exchange_chain_kernel,
        out_shape=(
            jax.ShapeDtypeStruct(xs.shape, xs.dtype),
            jax.ShapeDtypeStruct(gs.shape, gs.dtype),
            state,
            state,
        ),
        in_specs=[ANY, ANY, VMEM, VMEM, SMEM],
        out_specs=(ANY, ANY, VMEM, VMEM),
        scratch_shapes=[
            pltpu.VMEM(end_local.shape, jnp.bfloat16),
            pltpu.VMEM(end_local.shape, jnp.bfloat16),
            pltpu.SemaphoreType.DMA((2, count)),
            pltpu.SemaphoreType.DMA((2, count)),
            pltpu.SemaphoreType.DMA((2,)),
            pltpu.SemaphoreType.DMA((CHAIN_CHUNKS,)),
            pltpu.SemaphoreType.DMA((CHAIN_CHUNKS,)),
            pltpu.SemaphoreType.DMA((CHAIN_CHUNKS,)),
            pltpu.SemaphoreType.DMA((CHAIN_CHUNKS,)),
        ],
        compiler_params=pltpu.CompilerParams(collective_id=1, has_side_effects=True),
        name="exchange_chain",
    )(xs, gs, end_local, own_grad, decay)


def back_kernel(
    ts, bs, wp, ws, rt, rb, rp, rs, send, recv, own_sem, z_send, z_recv, z_own
):
    frame, row = lax.axis_index("frame"), lax.axis_index("row")
    count, bands = lax.axis_size("frame"), lax.axis_size("row")
    share = wp.shape[0] // bands
    barrier = pltpu.get_barrier_semaphore()
    each(1, count, lambda k: tell(barrier, frame=(frame + k) % count))
    each(1, bands, lambda k: tell(barrier, row=(row + k) % bands))
    pl.semaphore_wait(barrier, count - 1 + bands - 1)

    def pieces(j):
        start = pl.multiple_of(j * share, share)
        return (wp.at[pl.ds(start, share), :], rp), (ws.at[:, pl.ds(start, share)], rs)

    def z_out(i, k):
        peer = (row + k) % bands
        src, dst = pieces(peer)[i]
        return push(src, dst.at[row], z_send.at[i, k], z_recv.at[i, k], row=peer)

    def z_in(i, k):
        origin = (row + bands - k) % bands
        src, dst = pieces(origin)[i]
        return push(src, dst.at[origin], z_send.at[i, k], z_recv.at[i, k], row=origin)

    def z_self(i):
        src, dst = pieces(row)[i]
        return pltpu.make_async_copy(src, dst.at[row], z_own.at[i])

    for i in range(2):
        z_self(i).start()

    def begin(k):
        for i in range(2):
            z_out(i, k).start()

    each(1, bands, begin)
    plane_start(frame, count, [(ts, rt), (bs, rb)], send, recv, own_sem)
    plane_wait(frame, count, [(ts, rt), (bs, rb)], send, recv, own_sem)

    def end(k):
        for i in range(2):
            z_in(i, k).wait_recv()
            z_out(i, k).wait_send()

    each(1, bands, end)
    for i in range(2):
        z_self(i).wait()


def back(ts, bs, wp, ws):
    count, bands = lax.axis_size("frame"), lax.axis_size("row")
    share = wp.shape[0] // bands
    return pl.pallas_call(
        back_kernel,
        out_shape=(
            jax.ShapeDtypeStruct(ts.shape, ts.dtype),
            jax.ShapeDtypeStruct(bs.shape, bs.dtype),
            jax.ShapeDtypeStruct((bands, share, wp.shape[1]), wp.dtype),
            jax.ShapeDtypeStruct((bands, ws.shape[0], share), ws.dtype),
        ),
        in_specs=[ANY] * 4,
        out_specs=(ANY,) * 4,
        scratch_shapes=[
            pltpu.SemaphoreType.DMA((2, count)),
            pltpu.SemaphoreType.DMA((2, count)),
            pltpu.SemaphoreType.DMA((2,)),
            pltpu.SemaphoreType.DMA((2, bands)),
            pltpu.SemaphoreType.DMA((2, bands)),
            pltpu.SemaphoreType.DMA((2,)),
        ],
        compiler_params=pltpu.CompilerParams(collective_id=2, has_side_effects=True),
        name="back",
    )(ts, bs, wp, ws)


def plane_kernel(src, out, send, recv, own_sem):
    frame, count = lax.axis_index("frame"), lax.axis_size("frame")
    barrier = pltpu.get_barrier_semaphore()
    each(1, count, lambda k: tell(barrier, frame=(frame + k) % count))
    pl.semaphore_wait(barrier, count - 1)
    plane_start(frame, count, [(src, out)], send, recv, own_sem)
    plane_wait(frame, count, [(src, out)], send, recv, own_sem)


def plane(src):
    count = lax.axis_size("frame")
    return pl.pallas_call(
        plane_kernel,
        out_shape=jax.ShapeDtypeStruct(src.shape, src.dtype),
        in_specs=[VMEM],
        out_specs=VMEM,
        scratch_shapes=[
            pltpu.SemaphoreType.DMA((1, count)),
            pltpu.SemaphoreType.DMA((1, count)),
            pltpu.SemaphoreType.DMA((1,)),
        ],
        compiler_params=pltpu.CompilerParams(collective_id=3, has_side_effects=True),
        name="plane",
    )(src)


def deliver_kernel(weights, mods, rw, rm, w_send, w_recv, w_own, m_send, m_recv, m_own):
    frame, row = lax.axis_index("frame"), lax.axis_index("row")
    count, bands = lax.axis_size("frame"), lax.axis_size("row")
    per = count // bands
    home = row * per + frame // bands
    slot = frame % bands
    from_row, from_frame = frame // per, (frame % per) * bands
    barrier = pltpu.get_barrier_semaphore()

    def other(f, r):
        return jnp.logical_or(f != frame, r != row)

    def ready(i):
        @pl.when(other(from_frame + i, from_row))
        def _():
            tell(barrier, frame=from_frame + i, row=from_row)

    each(0, bands, ready)
    each(1, bands, lambda k: tell(barrier, row=(row + k) % bands))
    local = jnp.where(home == frame, 1, 0)
    pl.semaphore_wait(barrier, bands - local + bands - 1)

    def w_out(r):
        return push(weights, rw.at[slot], w_send.at[r], w_recv.at[slot], frame=home, row=r)

    def w_in(i):
        return push(weights, rw.at[i], w_send.at[i], w_recv.at[i], frame=from_frame + i, row=from_row)

    w_self = pltpu.make_async_copy(weights, rw.at[slot], w_own)
    m_self = pltpu.make_async_copy(mods, rm.at[row], m_own)
    m_self.start()

    def m_out(k):
        return push(mods, rm.at[row], m_send.at[k], m_recv.at[k], row=(row + k) % bands)

    def m_in(k):
        origin = (row + bands - k) % bands
        return push(mods, rm.at[origin], m_send.at[k], m_recv.at[k], row=origin)

    def start_weights(r):
        @pl.when(other(home, r))
        def _():
            w_out(r).start()

        @pl.when(jnp.logical_not(other(home, r)))
        def _():
            w_self.start()

    each(0, bands, start_weights)
    each(1, bands, lambda k: m_out(k).start())

    def end_weights(i):
        @pl.when(other(from_frame + i, from_row))
        def _():
            w_in(i).wait_recv()

        @pl.when(jnp.logical_not(other(from_frame + i, from_row)))
        def _():
            w_self.wait()

        @pl.when(other(home, i))
        def _():
            w_out(i).wait_send()

    each(0, bands, end_weights)

    def end_mods(k):
        m_in(k).wait_recv()
        m_out(k).wait_send()

    each(1, bands, end_mods)
    m_self.wait()


def deliver(weights, mods):
    bands = lax.axis_size("row")
    return pl.pallas_call(
        deliver_kernel,
        out_shape=(
            jax.ShapeDtypeStruct((bands, *weights.shape), weights.dtype),
            jax.ShapeDtypeStruct((bands, *mods.shape), mods.dtype),
        ),
        in_specs=[VMEM, VMEM],
        out_specs=(VMEM, VMEM),
        scratch_shapes=[
            pltpu.SemaphoreType.DMA((bands,)),
            pltpu.SemaphoreType.DMA((bands,)),
            pltpu.SemaphoreType.DMA,
            pltpu.SemaphoreType.DMA((bands,)),
            pltpu.SemaphoreType.DMA((bands,)),
            pltpu.SemaphoreType.DMA,
        ],
        compiler_params=pltpu.CompilerParams(collective_id=4, has_side_effects=True),
        name="deliver",
    )(weights, mods)


def time_embed(timestep, embed_dim):
    half_dim = embed_dim // 2
    frequency = jnp.exp(-math.log(10000.0) * jnp.arange(half_dim, dtype=jnp.float32) / half_dim)
    angles = timestep.astype(jnp.float32)[:, None] * frequency[None, :]
    return jax.nn.silu(jnp.concatenate([jnp.cos(angles), jnp.sin(angles)], axis=1))


def running_sum(values):
    length = values.shape[1]
    lower = jnp.tril(jnp.ones((length, length), jnp.float32))
    return jnp.einsum("tu,suh->sth", lower, values, precision=lax.Precision.HIGHEST)


def block_parts(normed, coeffs, logits, step_bias, decay_rate, need_end):
    seq_count, length, feat_width = normed.shape
    head_count = decay_rate.shape[0]
    inputs = normed.reshape(seq_count, length, head_count, feat_width // head_count)
    state_size = coeffs.shape[-1] // 2
    b_part = coeffs[..., :state_size]
    c_part = coeffs[..., state_size:]
    step_size = jax.nn.softplus(logits.astype(jnp.float32) + step_bias)
    cum_log = running_sum(-step_size * decay_rate)
    scores = (
        jnp.einsum("stn,sun->stu", c_part, b_part, preferred_element_type=jnp.float32) / state_size
    )
    lag_rows = jnp.swapaxes(cum_log, 1, 2)
    causal = jnp.tril(jnp.ones((length, length), dtype=bool))
    differences = lag_rows[:, :, :, None] - lag_rows[:, :, None, :]
    decays = jnp.where(causal, jnp.exp(jnp.where(causal, differences, 0.0)), 0.0)
    spread = jnp.swapaxes(step_size, 1, 2)
    weights = (scores[:, None, :, :] * decays * spread[:, :, None, :]).astype(jnp.bfloat16)
    inner_out = jnp.einsum("shtu,suhp->sthp", weights, inputs, preferred_element_type=jnp.float32)
    inner_out = inner_out.reshape(seq_count, length, feat_width)
    if need_end:
        end_log = cum_log[:, -1:, :]
        lead_decay = jnp.exp(end_log - cum_log) * step_size
        scaled = (inputs.astype(jnp.float32) * lead_decay[..., None]).astype(jnp.bfloat16)
        end_local = jnp.einsum("sthp,stn->shpn", scaled, b_part, preferred_element_type=jnp.float32)
    else:
        end_local = jnp.zeros(
            (seq_count, head_count, feat_width // head_count, state_size), jnp.float32
        )
    return (inner_out, end_local, cum_log, c_part)


def carry_term(cum_log, c_part, state_in):
    seq_count, length, head_count = cum_log.shape
    state_size = c_part.shape[-1]
    reached = jnp.einsum(
        "stn,shpn->sthp", c_part.astype(jnp.float32), state_in, precision=lax.Precision.HIGHEST
    )
    return (reached * jnp.exp(cum_log)[..., None] / state_size).reshape(seq_count, length, -1)


def three_parts(values):
    first = lax.reduce_precision(values, 8, 7)
    second = lax.reduce_precision(values - first, 8, 7)
    return first, second, values - first - second


def per_device(
    tokens,
    cotangent,
    timestep,
    mod_weight,
    proj_weight,
    step_weight,
    step_bias,
    rate_space,
    rate_time,
    skip_gain,
):
    frame_count = lax.axis_size("frame")
    row_count = lax.axis_size("row")
    frame_id = lax.axis_index("frame")
    feat_width = tokens.shape[-1]
    band_len = tokens.shape[1] * tokens.shape[2]
    clip_count = timestep.shape[0]
    clip_frames = frame_count // clip_count
    site_count = band_len // frame_count
    head_count = rate_space.shape[0]
    state_size = proj_weight.shape[1] // 2
    depth = proj_weight.shape[0]
    clip_id = frame_id // clip_frames
    factor = (frame_count * row_count * band_len) ** (-0.5)
    tokens = tokens.reshape(band_len, feat_width)
    flat_grad = cotangent.reshape(band_len, feat_width)

    activated = time_embed(timestep, mod_weight.shape[0]).astype(jnp.bfloat16)
    mod_cols = jnp.dot(activated, mod_weight, preferred_element_type=jnp.float32)
    lane = state_size
    mod_rows = [part.reshape(-1, lane).astype(jnp.bfloat16) for part in three_parts(mod_cols)]
    rows = [proj_weight[:, :state_size], proj_weight[:, state_size:], step_weight.reshape(-1, lane), *mod_rows]
    used = sum(r.shape[0] for r in rows)
    chunk = jnp.concatenate([*rows, jnp.zeros((-used % 16, lane), jnp.bfloat16)], axis=0)
    gathered = gather(chunk)
    b_weight = gathered[:, :depth].reshape(feat_width, state_size)
    c_weight = gathered[:, depth : 2 * depth].reshape(feat_width, state_size)
    proj_full = jnp.concatenate([b_weight, c_weight], axis=1)
    step_rows = depth * head_count // lane
    step_full = gathered[:, 2 * depth : 2 * depth + step_rows].reshape(feat_width, head_count)
    mod_height = mod_rows[0].shape[0]
    mod_parts = gathered[:, 2 * depth + step_rows : 2 * depth + step_rows + 3 * mod_height]
    mod_parts = mod_parts.astype(jnp.float32).reshape(frame_count, 3, clip_count, -1)
    modulation = mod_parts[:, 0] + mod_parts[:, 1] + mod_parts[:, 2]
    modulation = modulation.transpose(1, 0, 2).reshape(clip_count, 2 * feat_width)
    shift_all, scale_all = modulation[:, :feat_width], modulation[:, feat_width:]
    shift_vec = lax.dynamic_index_in_dim(shift_all, clip_id, 0, keepdims=False)
    scale_vec = lax.dynamic_index_in_dim(scale_all, clip_id, 0, keepdims=False)

    tokens_wide = tokens.astype(jnp.float32)
    inverse = lax.rsqrt(jnp.mean(tokens_wide * tokens_wide, axis=-1, keepdims=True) + norm_eps)
    unit_rows = tokens_wide * inverse
    normed = (unit_rows * (1.0 + scale_vec) + shift_vec).astype(jnp.bfloat16)
    projected = jnp.dot(normed, proj_full, preferred_element_type=jnp.float32).astype(jnp.bfloat16)
    logits = jnp.dot(normed, step_full, preferred_element_type=jnp.float32).astype(jnp.bfloat16)
    skip_full = jnp.repeat(skip_gain, feat_width // head_count)
    upstream = flat_grad.astype(jnp.float32)

    def space_parts(normed_band, proj_band, logit_band):
        return block_parts(normed_band, proj_band, logit_band, step_bias, rate_space, True)

    parts_out, parts_pull = jax.vjp(space_parts, normed[None], projected[None], logits[None])
    inner_out, end_local, cum_log, c_part = parts_out
    end_decay = jnp.exp(cum_log[:, -1, :])
    by_head = upstream.reshape(band_len, head_count, -1) * jnp.exp(cum_log[0])[..., None] / state_size
    own_grad = jnp.einsum(
        "thp,tn->hpn",
        by_head.astype(jnp.bfloat16),
        c_part[0],
        preferred_element_type=jnp.float32,
    )
    site_tokens, site_grad, state_in, later_grad = exchange_chain(
        tokens.reshape(frame_count, site_count, feat_width),
        flat_grad.reshape(frame_count, site_count, feat_width),
        end_local.reshape(feat_width, state_size),
        own_grad.reshape(feat_width, state_size),
        end_decay.reshape(head_count),
    )
    state_in = state_in.reshape(end_local.shape).astype(jnp.float32)
    later_grad = later_grad.reshape(end_local.shape).astype(jnp.float32)

    site_wide = site_tokens.astype(jnp.float32)
    site_unit = site_wide * lax.rsqrt(jnp.mean(site_wide * site_wide, axis=-1, keepdims=True) + norm_eps)
    by_clip = site_unit.reshape(clip_count, -1, feat_width)
    site_normed = (by_clip * (1.0 + scale_all[:, None, :]) + shift_all[:, None, :]).astype(jnp.bfloat16)
    site_normed = site_normed.reshape(frame_count * site_count, feat_width)
    site_proj = jnp.dot(site_normed, proj_full, preferred_element_type=jnp.float32).astype(jnp.bfloat16)
    site_logits = jnp.dot(site_normed, step_full, preferred_element_type=jnp.float32).astype(jnp.bfloat16)

    def to_seq(member):
        return member.reshape(frame_count, site_count, member.shape[-1]).transpose(1, 0, 2)

    def from_seq(member):
        return member.transpose(1, 0, 2).reshape(frame_count * site_count, member.shape[-1])

    def time_path(normed_seq, proj_seq, logit_seq):
        return block_parts(normed_seq, proj_seq, logit_seq, step_bias, rate_time, False)[0]

    time_out, time_pull = jax.vjp(time_path, to_seq(site_normed), to_seq(site_proj), to_seq(site_logits))
    time_dnorm, time_dproj, time_dlogit = time_pull(to_seq(site_grad).astype(jnp.float32))
    time_dnorm, time_dproj, time_dlogit = from_seq(time_dnorm), from_seq(time_dproj), from_seq(time_dlogit)
    time_back = (
        time_dnorm.astype(jnp.float32)
        + jnp.dot(time_dproj, proj_full.T, preferred_element_type=jnp.float32)
        + jnp.dot(time_dlogit, step_full.T, preferred_element_type=jnp.float32)
    ).astype(jnp.bfloat16)

    carried, carry_pull = jax.vjp(carry_term, cum_log, c_part, state_in)
    space_out = (inner_out + carried)[0]
    carry_dcum, carry_dc, unused = carry_pull(upstream[None])
    end_dlog = jnp.sum(later_grad * state_in, axis=(2, 3)) * end_decay
    carry_dcum = carry_dcum.at[:, -1, :].add(end_dlog)
    space_dnorm, space_dproj, space_dlogit = parts_pull(
        (upstream[None], later_grad, carry_dcum, carry_dc)
    )
    proj_term = jnp.dot(
        normed.T, space_dproj[0], preferred_element_type=jnp.float32
    ) + jnp.dot(site_normed.T, time_dproj, preferred_element_type=jnp.float32)
    step_term = jnp.dot(
        space_dlogit[0].T, normed, preferred_element_type=jnp.float32
    ) + jnp.dot(time_dlogit.T, site_normed, preferred_element_type=jnp.float32)
    frame_time, frame_back, proj_parts, step_parts = back(
        from_seq(time_out.astype(jnp.bfloat16)).reshape(frame_count, site_count, feat_width),
        time_back.reshape(frame_count, site_count, feat_width),
        proj_term.astype(jnp.bfloat16),
        step_term.astype(jnp.bfloat16),
    )
    frame_time = frame_time.reshape(band_len, feat_width)
    frame_back = frame_back.reshape(band_len, feat_width)
    mixed = (
        space_out + frame_time.astype(jnp.float32) + skip_full * normed.astype(jnp.float32)
    ).astype(jnp.bfloat16)
    skip_dnorm = (upstream * skip_full).astype(jnp.bfloat16)
    total_dnorm = space_dnorm[0] + skip_dnorm
    pre_grad = (
        total_dnorm.astype(jnp.float32)
        + jnp.dot(space_dproj[0], proj_full.T, preferred_element_type=jnp.float32)
        + jnp.dot(space_dlogit[0], step_full.T, preferred_element_type=jnp.float32)
        + frame_back.astype(jnp.float32)
    )
    shift_grad = jnp.sum(pre_grad, axis=0)
    scale_grad = jnp.sum(pre_grad * unit_rows, axis=0)
    unit_grad = pre_grad * (1.0 + scale_vec)
    d_tokens = inverse * (unit_grad - unit_rows * jnp.mean(unit_grad * unit_rows, axis=-1, keepdims=True))

    proj_sum = jnp.sum(proj_parts.astype(jnp.float32), axis=0).reshape(frame_count, -1)
    step_sum = jnp.sum(step_parts.astype(jnp.float32), axis=0).T.reshape(frame_count, -1)
    mod_term = jnp.concatenate([shift_grad, scale_grad]).reshape(frame_count, -1)
    payload = jnp.concatenate([proj_sum, step_sum, mod_term], axis=1)
    payload = jnp.pad(payload, ((0, 0), (0, -payload.shape[1] % (16 * lane))))
    arrived = plane(payload.reshape(frame_count, -1, lane).astype(jnp.bfloat16)).astype(jnp.float32)
    by_clip = jnp.sum(arrived.reshape(clip_count, clip_frames, *arrived.shape[1:]), axis=1)
    weight_sum = jnp.sum(by_clip, axis=0)
    mod_start = proj_sum.shape[1] + step_sum.shape[1]
    mod_width = mod_term.shape[1]
    mod_part = by_clip.reshape(clip_count, -1)[:, mod_start : mod_start + mod_width]
    mod_box = jnp.pad(mod_part, ((0, -clip_count % 8), (0, -mod_width % 128)))
    weight_box, mod_boxes = deliver(weight_sum, mod_box)
    weight_flat = weight_box.reshape(row_count, -1)
    grad_proj = weight_flat[:, : proj_sum.shape[1]].reshape(depth, 2 * state_size) * factor
    grad_step = weight_flat[:, proj_sum.shape[1] : mod_start].reshape(depth, head_count) * factor
    mod_sum = jnp.sum(mod_boxes, axis=0)[:clip_count, :mod_width]
    grad_mod = (
        jnp.dot(activated.astype(jnp.float32).T, mod_sum, precision=lax.Precision.HIGHEST) * factor
    )
    shape = cotangent.shape
    return (
        mixed.reshape(shape),
        d_tokens.astype(jnp.bfloat16).reshape(shape),
        grad_proj,
        grad_step,
        grad_mod,
    )


def solution(mesh):
    placed = (
        P("frame", "row", None, None),
        P("frame", "row", None, None),
        P(),
        P(None, "frame"),
        P("frame", None),
        P("frame", None),
        P(),
        P(),
        P(),
        P(),
    )
    return jax.shard_map(
        per_device,
        mesh=mesh,
        in_specs=placed,
        out_specs=(
            P("frame", "row", None, None),
            P("frame", "row", None, None),
            P("frame", None),
            P("frame", None),
            P(None, "frame"),
        ),
        check_vma=False,
    )
```

```python
import functools
import math

import jax
import jax.numpy as jnp
from jax import lax
from jax.experimental import pallas as pl
from jax.experimental.pallas import tpu as pltpu
from jax.sharding import PartitionSpec as P

norm_eps = 1e-05
MESH = pl.DeviceIdType.MESH
ANY = pl.BlockSpec(memory_space=pl.ANY)
VMEM = pl.BlockSpec(memory_space=pltpu.VMEM)
SMEM = pl.BlockSpec(memory_space=pltpu.SMEM)
CHAIN_CHUNKS = 16
CHAIN_LAG = 6
PLANE_WIDE = 4
PLANE_AHEAD = 8
PLANE_LATEST = 24


def at(frame=None, row=None):
    place = {}
    if frame is not None:
        place["frame"] = frame
    if row is not None:
        place["row"] = row
    return place


def tell(sem, **place):
    pl.semaphore_signal(sem, inc=1, device_id=at(**place), device_id_type=MESH)


def push(src, dst, send_sem, recv_sem, **place):
    return pltpu.make_async_remote_copy(
        src_ref=src,
        dst_ref=dst,
        send_sem=send_sem,
        recv_sem=recv_sem,
        device_id=at(**place),
        device_id_type=MESH,
    )


def each(start, stop, body):
    def step(k, carry):
        body(k)
        return carry

    lax.fori_loop(start, stop, step, 0)


def gather_kernel(src, out, y_send, y_recv, x_send, x_recv, c_send, c_recv, local_sem):
    high, wide = out.shape[0], out.shape[1]
    frame = lax.axis_index("frame")
    core, x, y = frame % 2, frame // 2 % wide, frame // (2 * wide)

    def index(y, x, core):
        return (y * wide + x) * 2 + core

    sibling = index(y, x, 1 - core)
    barrier = pltpu.get_barrier_semaphore()
    for k in range(1, high):
        tell(barrier, frame=index((y + k) % high, x, core))
    for k in range(1, wide):
        tell(barrier, frame=index(y, (x + k) % wide, core))
    tell(barrier, frame=sibling)
    own = pltpu.make_async_copy(src, out.at[y, x, core], local_sem)
    own.start()
    pl.semaphore_wait(barrier, high + wide - 1)

    def along_y(k, back=False):
        place = (y + high - k) % high if back else y
        peer = index((y + k) % high, x, core)
        return push(src, out.at[place, x, core], y_send.at[k], y_recv.at[k], frame=peer)

    def along_x(k, i, back=False):
        place = (y + high - k) % high
        held = src if k == 0 else out.at[place, x, core]
        column = (x + wide - i) % wide if back else x
        return push(
            held, out.at[place, column, core], x_send.at[k, i], x_recv.at[k, i],
            frame=index(y, (x + i) % wide, core),
        )

    def across(k, back=False):
        place = (y + high - k) % high
        side = 1 - core if back else core
        held = out.at[place, :, side]
        return push(out.at[place, :, core], held, c_send.at[k], c_recv.at[k], frame=sibling)

    near = sorted(range(1, high), key=lambda k: min(k, high - k))
    for k in near:
        along_y(k).start()
    for i in range(1, wide):
        along_x(0, i).start()
    for k in near:
        along_y(k, True).wait_recv()
        for i in range(1, wide):
            along_x(k, i).start()
    own.wait()
    for k in [0, *near]:
        for i in range(1, wide):
            along_x(k, i, True).wait_recv()
        across(k).start()
    for k in [0, *near]:
        across(k, True).wait_recv()
    for k in near:
        along_y(k).wait_send()
    for k in [0, *near]:
        for i in range(1, wide):
            along_x(k, i).wait_send()
        across(k).wait_send()


def gather(chunk):
    count = lax.axis_size("frame")
    wide = PLANE_WIDE
    high = count // (2 * wide)
    out = pl.pallas_call(
        gather_kernel,
        out_shape=jax.ShapeDtypeStruct((high, wide, 2, *chunk.shape), chunk.dtype),
        in_specs=[VMEM],
        out_specs=VMEM,
        scratch_shapes=[
            pltpu.SemaphoreType.DMA((high,)),
            pltpu.SemaphoreType.DMA((high,)),
            pltpu.SemaphoreType.DMA((high, wide)),
            pltpu.SemaphoreType.DMA((high, wide)),
            pltpu.SemaphoreType.DMA((high,)),
            pltpu.SemaphoreType.DMA((high,)),
            pltpu.SemaphoreType.DMA,
        ],
        compiler_params=pltpu.CompilerParams(collective_id=0, has_side_effects=True),
        name="gather",
    )(chunk)
    return out.reshape(count, *chunk.shape)


def plane_copies(frame, count, pairs, send, recv):
    def out_piece(i, k):
        peer = (frame + k) % count
        src, dst = pairs[i]
        return push(src.at[peer], dst.at[frame], send.at[i, k], recv.at[i, k], frame=peer)

    def in_piece(i, k):
        origin = (frame + count - k) % count
        src, dst = pairs[i]
        return push(src.at[origin], dst.at[origin], send.at[i, k], recv.at[i, k], frame=origin)

    return out_piece, in_piece


def plane_start(frame, count, pairs, send, recv, own_sem, some=None):
    out_piece, unused = plane_copies(frame, count, pairs, send, recv)
    for i, (src, dst) in enumerate(pairs):
        pltpu.make_async_copy(src.at[frame], dst.at[frame], own_sem.at[i]).start()

    def begin(k):
        for i in range(len(pairs)):
            out_piece(i, k).start()

    each(1, count if some is None else some, begin)
    return begin


def plane_wait(frame, count, pairs, send, recv, own_sem):
    out_piece, in_piece = plane_copies(frame, count, pairs, send, recv)

    def end(k):
        for i in range(len(pairs)):
            in_piece(i, k).wait_recv()
            out_piece(i, k).wait_send()

    each(1, count, end)
    for i, (src, dst) in enumerate(pairs):
        pltpu.make_async_copy(src.at[frame], dst.at[frame], own_sem.at[i]).wait()


def exchange_chain_kernel(
    xs, gs, end_local, own_grad, decay, rx, rg, state_in, later, fwd_out, bwd_out, send, recv, own_sem,
    fwd_send, fwd_recv, bwd_send, bwd_recv,
):
    frame, row = lax.axis_index("frame"), lax.axis_index("row")
    count, bands = lax.axis_size("frame"), lax.axis_size("row")
    height = end_local.shape[0] // CHAIN_CHUNKS
    heads = decay.shape[0]
    per_head = end_local.shape[0] // heads
    barrier = pltpu.get_barrier_semaphore()
    each(1, count, lambda k: tell(barrier, frame=(frame + k) % count))

    @pl.when(row > 0)
    def _():
        tell(barrier, row=row - 1)

    @pl.when(row < bands - 1)
    def _():
        tell(barrier, row=row + 1)

    neighbours = jnp.where(row > 0, 1, 0) + jnp.where(row < bands - 1, 1, 0)
    pl.semaphore_wait(barrier, count - 1 + neighbours)

    def rows_of(c):
        return pl.ds(pl.multiple_of(c * height, height), height)

    def fwd(c):
        where = rows_of(c)
        return push(fwd_out.at[where], state_in.at[where], fwd_send.at[c], fwd_recv.at[c], row=row + 1)

    def bwd(c):
        where = rows_of(c)
        return push(bwd_out.at[where], later.at[where], bwd_send.at[c], bwd_recv.at[c], row=row - 1)

    def fwd_in(c):
        where = rows_of(c)
        return push(fwd_out.at[where], state_in.at[where], fwd_send.at[c], fwd_recv.at[c], row=row - 1)

    def bwd_in(c):
        where = rows_of(c)
        return push(bwd_out.at[where], later.at[where], bwd_send.at[c], bwd_recv.at[c], row=row + 1)

    def join(c, before, own, result):
        for j in range(height // per_head):
            where = pl.ds(pl.multiple_of(c * height + j * per_head, per_head), per_head)
            factor = decay[c * (height // per_head) + j]
            result[where, :] = (
                before[where, :].astype(jnp.float32) * factor + own[where, :]
            ).astype(result.dtype)

    @pl.when(row == 0)
    def _():
        state_in[...] = jnp.zeros_like(state_in)
        for c in range(CHAIN_CHUNKS):
            fwd_out[rows_of(c), :] = end_local[rows_of(c), :].astype(fwd_out.dtype)
            fwd(c).start()

    @pl.when(row == bands - 1)
    def _():
        later[...] = jnp.zeros_like(later)
        for c in range(CHAIN_CHUNKS):
            bwd_out[rows_of(c), :] = own_grad[rows_of(c), :].astype(bwd_out.dtype)
            bwd(c).start()

    slots = CHAIN_CHUNKS + (bands - 1) * CHAIN_LAG
    ahead = 1 + PLANE_AHEAD
    per_slot = -(-(count - ahead) // (slots - PLANE_LATEST))
    begin = plane_start(frame, count, [(xs, rx), (gs, rg)], send, recv, own_sem, ahead)

    def slot(s):
        f = s - row * CHAIN_LAG
        b = s - (bands - 1 - row) * CHAIN_LAG

        @pl.when(jnp.logical_and(row > 0, jnp.logical_and(f >= 0, f < CHAIN_CHUNKS)))
        def _():
            fwd_in(f).wait_recv()

            @pl.when(row < bands - 1)
            def _():
                join(f, state_in, end_local, fwd_out)
                fwd(f).start()

        @pl.when(jnp.logical_and(row < bands - 1, jnp.logical_and(b >= 0, b < CHAIN_CHUNKS)))
        def _():
            bwd_in(b).wait_recv()

            @pl.when(row > 0)
            def _():
                join(b, later, own_grad, bwd_out)
                bwd(b).start()

        first = jnp.minimum(ahead + s * per_slot, count)
        each(first, jnp.minimum(first + per_slot, count), begin)

    each(0, slots, slot)
    plane_wait(frame, count, [(xs, rx), (gs, rg)], send, recv, own_sem)

    @pl.when(row < bands - 1)
    def _():
        for c in range(CHAIN_CHUNKS):
            fwd(c).wait_send()

    @pl.when(row > 0)
    def _():
        for c in range(CHAIN_CHUNKS):
            bwd(c).wait_send()


def exchange_chain(xs, gs, end_local, own_grad, decay):
    count = lax.axis_size("frame")
    state = jax.ShapeDtypeStruct(end_local.shape, jnp.bfloat16)
    return pl.pallas_call(
        exchange_chain_kernel,
        out_shape=(
            jax.ShapeDtypeStruct(xs.shape, xs.dtype),
            jax.ShapeDtypeStruct(gs.shape, gs.dtype),
            state,
            state,
        ),
        in_specs=[ANY, ANY, VMEM, VMEM, SMEM],
        out_specs=(ANY, ANY, VMEM, VMEM),
        scratch_shapes=[
            pltpu.VMEM(end_local.shape, jnp.bfloat16),
            pltpu.VMEM(end_local.shape, jnp.bfloat16),
            pltpu.SemaphoreType.DMA((2, count)),
            pltpu.SemaphoreType.DMA((2, count)),
            pltpu.SemaphoreType.DMA((2,)),
            pltpu.SemaphoreType.DMA((CHAIN_CHUNKS,)),
            pltpu.SemaphoreType.DMA((CHAIN_CHUNKS,)),
            pltpu.SemaphoreType.DMA((CHAIN_CHUNKS,)),
            pltpu.SemaphoreType.DMA((CHAIN_CHUNKS,)),
        ],
        compiler_params=pltpu.CompilerParams(collective_id=1, has_side_effects=True),
        name="exchange_chain",
    )(xs, gs, end_local, own_grad, decay)


def back_kernel(
    ts, bs, wg, rt, rb, rw, send, recv, own_sem, z_send, z_recv, z_own
):
    frame, row = lax.axis_index("frame"), lax.axis_index("row")
    count, bands = lax.axis_size("frame"), lax.axis_size("row")
    share = wg.shape[1] // bands
    barrier = pltpu.get_barrier_semaphore()
    each(1, count, lambda k: tell(barrier, frame=(frame + k) % count))
    each(1, bands, lambda k: tell(barrier, row=(row + k) % bands))
    pl.semaphore_wait(barrier, count - 1 + bands - 1)

    def piece(j):
        return wg.at[:, pl.ds(pl.multiple_of(j * share, share), share)]

    def z_out(k):
        peer = (row + k) % bands
        return push(piece(peer), rw.at[row], z_send.at[k], z_recv.at[k], row=peer)

    def z_in(k):
        origin = (row + bands - k) % bands
        return push(piece(origin), rw.at[origin], z_send.at[k], z_recv.at[k], row=origin)

    z_self = pltpu.make_async_copy(piece(row), rw.at[row], z_own)
    z_self.start()
    each(1, bands, lambda k: z_out(k).start())
    plane_start(frame, count, [(ts, rt), (bs, rb)], send, recv, own_sem)
    plane_wait(frame, count, [(ts, rt), (bs, rb)], send, recv, own_sem)

    def end(k):
        z_in(k).wait_recv()
        z_out(k).wait_send()

    each(1, bands, end)
    z_self.wait()


def back(ts, bs, wg):
    count, bands = lax.axis_size("frame"), lax.axis_size("row")
    share = wg.shape[1] // bands
    return pl.pallas_call(
        back_kernel,
        out_shape=(
            jax.ShapeDtypeStruct(ts.shape, ts.dtype),
            jax.ShapeDtypeStruct(bs.shape, bs.dtype),
            jax.ShapeDtypeStruct((bands, wg.shape[0], share), wg.dtype),
        ),
        in_specs=[ANY] * 3,
        out_specs=(ANY,) * 3,
        scratch_shapes=[
            pltpu.SemaphoreType.DMA((2, count)),
            pltpu.SemaphoreType.DMA((2, count)),
            pltpu.SemaphoreType.DMA((2,)),
            pltpu.SemaphoreType.DMA((bands,)),
            pltpu.SemaphoreType.DMA((bands,)),
            pltpu.SemaphoreType.DMA,
        ],
        compiler_params=pltpu.CompilerParams(collective_id=2, has_side_effects=True),
        name="back",
    )(ts, bs, wg)


def plane_kernel(src, out, send, recv, own_sem):
    frame, count = lax.axis_index("frame"), lax.axis_size("frame")
    barrier = pltpu.get_barrier_semaphore()
    each(1, count, lambda k: tell(barrier, frame=(frame + k) % count))
    pl.semaphore_wait(barrier, count - 1)
    plane_start(frame, count, [(src, out)], send, recv, own_sem)
    plane_wait(frame, count, [(src, out)], send, recv, own_sem)


def plane(src):
    count = lax.axis_size("frame")
    return pl.pallas_call(
        plane_kernel,
        out_shape=jax.ShapeDtypeStruct(src.shape, src.dtype),
        in_specs=[VMEM],
        out_specs=VMEM,
        scratch_shapes=[
            pltpu.SemaphoreType.DMA((1, count)),
            pltpu.SemaphoreType.DMA((1, count)),
            pltpu.SemaphoreType.DMA((1,)),
        ],
        compiler_params=pltpu.CompilerParams(collective_id=3, has_side_effects=True),
        name="plane",
    )(src)


def deliver_kernel(weights, mods, rw, rm, w_send, w_recv, w_own, m_send, m_recv, m_own):
    frame, row = lax.axis_index("frame"), lax.axis_index("row")
    count, bands = lax.axis_size("frame"), lax.axis_size("row")
    per = count // bands
    home = row * per + frame // bands
    slot = frame % bands
    from_row, from_frame = frame // per, (frame % per) * bands
    barrier = pltpu.get_barrier_semaphore()

    def other(f, r):
        return jnp.logical_or(f != frame, r != row)

    def ready(i):
        @pl.when(other(from_frame + i, from_row))
        def _():
            tell(barrier, frame=from_frame + i, row=from_row)

    each(0, bands, ready)
    each(1, bands, lambda k: tell(barrier, row=(row + k) % bands))
    local = jnp.where(home == frame, 1, 0)
    pl.semaphore_wait(barrier, bands - local + bands - 1)

    def w_out(r):
        return push(weights, rw.at[slot], w_send.at[r], w_recv.at[slot], frame=home, row=r)

    def w_in(i):
        return push(weights, rw.at[i], w_send.at[i], w_recv.at[i], frame=from_frame + i, row=from_row)

    w_self = pltpu.make_async_copy(weights, rw.at[slot], w_own)
    m_self = pltpu.make_async_copy(mods, rm.at[row], m_own)
    m_self.start()

    def m_out(k):
        return push(mods, rm.at[row], m_send.at[k], m_recv.at[k], row=(row + k) % bands)

    def m_in(k):
        origin = (row + bands - k) % bands
        return push(mods, rm.at[origin], m_send.at[k], m_recv.at[k], row=origin)

    def start_weights(r):
        @pl.when(other(home, r))
        def _():
            w_out(r).start()

        @pl.when(jnp.logical_not(other(home, r)))
        def _():
            w_self.start()

    each(0, bands, start_weights)
    each(1, bands, lambda k: m_out(k).start())

    def end_weights(i):
        @pl.when(other(from_frame + i, from_row))
        def _():
            w_in(i).wait_recv()

        @pl.when(jnp.logical_not(other(from_frame + i, from_row)))
        def _():
            w_self.wait()

        @pl.when(other(home, i))
        def _():
            w_out(i).wait_send()

    each(0, bands, end_weights)

    def end_mods(k):
        m_in(k).wait_recv()
        m_out(k).wait_send()

    each(1, bands, end_mods)
    m_self.wait()


def deliver(weights, mods):
    bands = lax.axis_size("row")
    return pl.pallas_call(
        deliver_kernel,
        out_shape=(
            jax.ShapeDtypeStruct((bands, *weights.shape), weights.dtype),
            jax.ShapeDtypeStruct((bands, *mods.shape), mods.dtype),
        ),
        in_specs=[VMEM, VMEM],
        out_specs=(VMEM, VMEM),
        scratch_shapes=[
            pltpu.SemaphoreType.DMA((bands,)),
            pltpu.SemaphoreType.DMA((bands,)),
            pltpu.SemaphoreType.DMA,
            pltpu.SemaphoreType.DMA((bands,)),
            pltpu.SemaphoreType.DMA((bands,)),
            pltpu.SemaphoreType.DMA,
        ],
        compiler_params=pltpu.CompilerParams(collective_id=4, has_side_effects=True),
        name="deliver",
    )(weights, mods)


def time_embed(timestep, embed_dim):
    half_dim = embed_dim // 2
    frequency = jnp.exp(-math.log(10000.0) * jnp.arange(half_dim, dtype=jnp.float32) / half_dim)
    angles = timestep.astype(jnp.float32)[:, None] * frequency[None, :]
    return jax.nn.silu(jnp.concatenate([jnp.cos(angles), jnp.sin(angles)], axis=1))


def halves(values):
    high = values.astype(jnp.bfloat16)
    return high, (values - high.astype(jnp.float32)).astype(jnp.bfloat16)


def mm(a, b):
    return jnp.dot(a, b, preferred_element_type=jnp.float32)


def mm_nt(a, b):
    return lax.dot_general(a, b, (((1,), (1,)), ((), ())), preferred_element_type=jnp.float32)


def mm_tn(a, b):
    return lax.dot_general(a, b, (((0,), (0,)), ((), ())), preferred_element_type=jnp.float32)


def with_ones(ones, values, dot):
    first = values.astype(jnp.bfloat16)
    rest = values - first.astype(jnp.float32)
    second = rest.astype(jnp.bfloat16)
    third = (rest - second.astype(jnp.float32)).astype(jnp.bfloat16)
    return dot(ones, first) + dot(ones, second) + dot(ones, third)


def earlier_mask(length, sites):
    t = lax.broadcasted_iota(jnp.int32, (length, length), 0)
    u = lax.broadcasted_iota(jnp.int32, (length, length), 1)
    return jnp.logical_and(u <= t, lax.rem(t, sites) == lax.rem(u, sites))


def steps_of(logits, bias, rate, mask):
    raised = logits.astype(jnp.float32) + bias
    step = jnp.maximum(raised, 0.0) + jnp.log1p(jnp.exp(-jnp.abs(raised)))
    lower = jnp.where(mask, 1.0, 0.0).astype(jnp.bfloat16)
    return raised, step, with_ones(lower, -step * rate, mm)


def spread(values, expand, where):
    high, low = halves(values)
    return mm(high, expand[:, where]) + mm(low, expand[:, where])


def per_head(values, collect, where):
    high, low = halves(values)
    return mm(high, collect[where, :]) + mm(low, collect[where, :])


def head_kernel(
    tokens, grad, weights, step_w, shift, scale, bias, rate, expand,
    normed_out, coeff_out, logit_out, end_out, own_out, decay_out,
):
    length, width = tokens.shape
    lanes = step_w.shape[1]
    values = tokens[...].astype(jnp.float32)
    inverse = lax.rsqrt(jnp.mean(values * values, axis=1, keepdims=True) + norm_eps)
    normed_out[...] = (values * inverse * (1.0 + scale[...]) + shift[...]).astype(jnp.bfloat16)
    project(normed_out, weights, step_w, coeff_out, logit_out)
    b_part, c_part = coeff_out[:, :lanes], coeff_out[:, lanes:]
    mask = earlier_mask(length, 1)
    unused, step, log = steps_of(logit_out[...], bias[...], rate[...], mask)
    last = log[length - 1 :, :]
    decay_out[...] = jnp.exp(last)
    lead = jnp.exp(last - log) * step
    reach = jnp.exp(log) * (1.0 / lanes)
    for j in range(width // lanes):
        where = slice(j * lanes, (j + 1) * lanes)
        scaled = (normed_out[:, where].astype(jnp.float32) * spread(lead, expand, where)).astype(jnp.bfloat16)
        end_out[where, :] = mm_tn(scaled, b_part)
        pulled = (grad[:, where].astype(jnp.float32) * spread(reach, expand, where)).astype(jnp.bfloat16)
        own_out[where, :] = mm_tn(pulled, c_part)


def project(normed, weights, step_w, coeff_out, logit_out):
    lanes = step_w.shape[1]
    depth = weights.shape[1] // 2
    count = weights.shape[0]
    for i in range(2):
        w = weights[:, i * depth : (i + 1) * depth, :].reshape(count * depth, lanes)
        coeff_out[:, i * lanes : (i + 1) * lanes] = mm(normed[...], w).astype(jnp.bfloat16)
    logit_out[...] = mm(normed[...], step_w[...]).astype(jnp.bfloat16)


def scan_pass(
    x_ref, g_ref, coeffs, logits, bias, rate, weights, step_w, expand, collect, skip, state, later,
    mixed_ref, dx_ref, back_ref, wg_ref, sites, first,
):
    length, width = x_ref.shape
    lanes = coeffs.shape[1] // 2
    space = state is not None
    b_part, c_part = coeffs[:, :lanes], coeffs[:, lanes:]
    mask = earlier_mask(length, sites)
    raised, step, log = steps_of(logits[...], bias[...], rate[...], mask)
    log_t = log.T
    scores = jnp.where(mask, mm_nt(c_part, b_part) * (1.0 / lanes), 0.0)
    left = lax.broadcasted_iota(jnp.int32, (length, lanes), 1) < lanes // 2
    d_scores = jnp.zeros((length, length), jnp.float32)
    pull_out = jnp.zeros((length, lanes), jnp.float32)
    pull_in = jnp.zeros((length, lanes), jnp.float32)
    d_b = jnp.zeros((length, lanes), jnp.float32)
    d_c = jnp.zeros((length, lanes), jnp.float32)
    if space:
        last = log[length - 1 :, :]
        reach_all = jnp.exp(log) * (1.0 / lanes)
        fade_all = jnp.exp(last - log)
        d_last = jnp.zeros((8, lanes), jnp.float32)
        state_rows = []
    for j in range(width // lanes):
        where = slice(j * lanes, (j + 1) * lanes)
        x, g = x_ref[:, where], g_ref[:, where]
        wide_x, wide_g = x.astype(jnp.float32), g.astype(jnp.float32)
        step_x = spread(step, expand, where)
        stepped_wide = wide_x * step_x
        stepped = stepped_wide.astype(jnp.bfloat16)
        outs, backs = [], []
        for i in range(2):
            h = 2 * j + i
            fall = jnp.exp(jnp.minimum(log[:, h : h + 1] - log_t[h : h + 1, :], 0.0))
            w = (scores * fall).astype(jnp.bfloat16)
            outs.append(mm(w, stepped))
            backs.append(mm_tn(w, g))
            own_half = left if i == 0 else jnp.logical_not(left)
            half_g = jnp.where(own_half, wide_g, 0.0).astype(jnp.bfloat16)
            d_scores += mm_nt(half_g, stepped) * fall
        out = jnp.where(left, outs[0], outs[1])
        d_step_x = jnp.where(left, backs[0], backs[1])
        if space:
            held, late = state[where, :], later[where, :]
            reach = spread(reach_all, expand, where)
            fade = spread(fade_all, expand, where)
            out += mm_nt(c_part, held) * reach
            d_c += mm((wide_g * reach).astype(jnp.bfloat16), held)
            from_end = mm_nt(b_part, late) * fade
            d_step_x += from_end
            d_b += mm((stepped_wide * fade).astype(jnp.bfloat16), late)
            to_last = jnp.sum(stepped_wide * from_end, axis=0, keepdims=True)
            d_last += per_head(jnp.broadcast_to(to_last, (8, lanes)), collect, where)
            both = held.astype(jnp.float32) * late.astype(jnp.float32)
            half = lanes // 2
            state_rows += [
                jnp.sum(both[:half], axis=0, keepdims=True),
                jnp.sum(both[half:], axis=0, keepdims=True),
            ]
            mixed_ref[:, where] = out + skip[:, where] * wide_x
            direct = (wide_g * skip[:, where]).astype(jnp.bfloat16).astype(jnp.float32)
            dx_ref[:, where] = step_x * d_step_x + direct
        else:
            mixed_ref[:, where] = out.astype(mixed_ref.dtype)
            dx_ref[:, where] = step_x * d_step_x
        pull_out += per_head(wide_g * out, collect, where)
        pull_in += per_head(wide_x * d_step_x, collect, where)
    d_low = (jnp.where(mask, d_scores, 0.0) * (1.0 / lanes)).astype(jnp.bfloat16)
    d_c += mm(d_low, b_part)
    d_b += mm_tn(d_low, c_part)
    d_log = pull_out - step * pull_in
    if space:
        states = jnp.concatenate([*state_rows, jnp.zeros((lanes - len(state_rows), lanes), jnp.float32)], axis=0)
        high, low = halves(states)
        ones = jnp.ones((8, lanes), jnp.bfloat16)
        d_last += (mm_nt(ones, high) + mm_nt(ones, low)) * jnp.exp(last)
        at_end = lax.broadcasted_iota(jnp.int32, (length, lanes), 0) == length - 1
        d_log += jnp.where(at_end, d_last[:1, :], 0.0)
    lower = jnp.where(mask, 1.0, 0.0).astype(jnp.bfloat16)
    d_fall = with_ones(lower, d_log, mm_tn)
    d_step = pull_in - rate[...] * d_fall
    d_logit = (d_step * jax.nn.sigmoid(raised)).astype(jnp.bfloat16)
    low_b, low_c = d_b.astype(jnp.bfloat16), d_c.astype(jnp.bfloat16)
    count, depth = weights.shape[0], weights.shape[1] // 2
    block = 8
    for k in range(count // block):
        cols = slice(k * block * depth, (k + 1) * block * depth)
        w_b = weights[k * block : (k + 1) * block, :depth, :].reshape(block * depth, lanes)
        w_c = weights[k * block : (k + 1) * block, depth:, :].reshape(block * depth, lanes)
        total = (
            dx_ref[:, cols] + mm_nt(low_b, w_b) + mm_nt(low_c, w_c) + mm_nt(d_logit, step_w[cols, :])
        )
        back_ref[:, cols] = total.astype(back_ref.dtype)
        x = x_ref[:, cols]
        heads = wg_ref.shape[0] - 2 * lanes
        terms = (mm_tn(low_b, x), mm_tn(low_c, x), mm_tn(d_logit, x)[:heads])
        for i, term in enumerate(terms):
            rows = slice(i * lanes, i * lanes + term.shape[0])
            wg_ref[rows, cols] = term if first else wg_ref[rows, cols] + term


def core_kernel(
    normed, grad, coeffs, logits, state, later, site_tokens, site_grad, weights, step_w, shift_all, scale_all,
    bias, rate_space, rate_time, skip, expand, collect,
    mixed_out, pre_out, time_out, back_out, wg_out, site_normed, site_coeffs, site_logits, dx, wg,
):
    length, width = normed.shape
    clips = shift_all.shape[0]
    sites = length // weights.shape[0]
    part = length // clips
    for c in range(clips):
        rows = slice(c * part, (c + 1) * part)
        values = site_tokens[rows, :].astype(jnp.float32)
        inverse = lax.rsqrt(jnp.mean(values * values, axis=1, keepdims=True) + norm_eps)
        site_normed[rows, :] = (
            values * inverse * (1.0 + scale_all[c : c + 1, :]) + shift_all[c : c + 1, :]
        ).astype(jnp.bfloat16)
    project(site_normed, weights, step_w, site_coeffs, site_logits)
    scan_pass(
        site_normed, site_grad, site_coeffs, site_logits, bias, rate_time, weights, step_w, expand, collect,
        None, None, None, time_out, dx, back_out, wg, sites, True,
    )
    scan_pass(
        normed, grad, coeffs, logits, bias, rate_space, weights, step_w, expand, collect,
        skip, state, later, mixed_out, dx, pre_out, wg, 1, False,
    )
    wg_out[...] = wg[...].astype(jnp.bfloat16)


BIG = 56 * 2**20


def head(tokens, grad, weights, step_w, shift, scale, bias, rate, expand):
    length, width = tokens.shape
    lanes = step_w.shape[1]
    low = functools.partial(jax.ShapeDtypeStruct, dtype=jnp.bfloat16)
    wide = functools.partial(jax.ShapeDtypeStruct, dtype=jnp.float32)
    return pl.pallas_call(
        head_kernel,
        out_shape=(
            low((length, width)),
            low((length, 2 * lanes)),
            low((length, lanes)),
            wide((width, lanes)),
            wide((width, lanes)),
            wide((1, lanes)),
        ),
        in_specs=[VMEM] * 9,
        out_specs=(VMEM,) * 6,
        compiler_params=pltpu.CompilerParams(vmem_limit_bytes=BIG),
        name="head",
    )(tokens, grad, weights, step_w, shift, scale, bias, rate, expand)


def core(heads, *operands):
    normed, coeffs, weights = operands[0], operands[2], operands[8]
    length, width = normed.shape
    lanes = coeffs.shape[1] // 2
    low = functools.partial(jax.ShapeDtypeStruct, dtype=jnp.bfloat16)
    wide = functools.partial(jax.ShapeDtypeStruct, dtype=jnp.float32)
    rows = 2 * lanes + heads
    return pl.pallas_call(
        core_kernel,
        out_shape=(
            wide((length, width)),
            wide((length, width)),
            low((length, width)),
            low((length, width)),
            low((rows, width)),
        ),
        in_specs=[VMEM] * 18,
        out_specs=(VMEM,) * 5,
        scratch_shapes=[
            pltpu.VMEM((length, width), jnp.bfloat16),
            pltpu.VMEM((length, 2 * lanes), jnp.bfloat16),
            pltpu.VMEM((length, lanes), jnp.bfloat16),
            pltpu.VMEM((length, width), jnp.float32),
            pltpu.VMEM((rows, width), jnp.float32),
        ],
        compiler_params=pltpu.CompilerParams(vmem_limit_bytes=BIG),
        name="core",
    )(*operands)


def three_parts(values):
    first = lax.reduce_precision(values, 8, 7)
    second = lax.reduce_precision(values - first, 8, 7)
    return first, second, values - first - second


def per_device(
    tokens,
    cotangent,
    timestep,
    mod_weight,
    proj_weight,
    step_weight,
    step_bias,
    rate_space,
    rate_time,
    skip_gain,
):
    frame_count = lax.axis_size("frame")
    row_count = lax.axis_size("row")
    frame_id = lax.axis_index("frame")
    feat_width = tokens.shape[-1]
    band_len = tokens.shape[1] * tokens.shape[2]
    clip_count = timestep.shape[0]
    clip_frames = frame_count // clip_count
    site_count = band_len // frame_count
    head_count = rate_space.shape[0]
    state_size = proj_weight.shape[1] // 2
    depth = proj_weight.shape[0]
    clip_id = frame_id // clip_frames
    factor = (frame_count * row_count * band_len) ** (-0.5)
    tokens = tokens.reshape(band_len, feat_width)
    flat_grad = cotangent.reshape(band_len, feat_width)

    activated = time_embed(timestep, mod_weight.shape[0]).astype(jnp.bfloat16)
    mod_cols = jnp.dot(activated, mod_weight, preferred_element_type=jnp.float32)
    lane = state_size
    mod_rows = [part.reshape(-1, lane).astype(jnp.bfloat16) for part in three_parts(mod_cols)]
    rows = [proj_weight[:, :state_size], proj_weight[:, state_size:], step_weight.reshape(-1, lane), *mod_rows]
    used = sum(r.shape[0] for r in rows)
    chunk = jnp.concatenate([*rows, jnp.zeros((-used % 16, lane), jnp.bfloat16)], axis=0)
    gathered = gather(chunk)
    weights = gathered[:, : 2 * depth]
    step_rows = depth * head_count // lane
    step_full = gathered[:, 2 * depth : 2 * depth + step_rows].reshape(feat_width, head_count)
    step_w = jnp.pad(step_full, ((0, 0), (0, lane - head_count)))
    mod_height = mod_rows[0].shape[0]
    mod_parts = gathered[:, 2 * depth + step_rows : 2 * depth + step_rows + 3 * mod_height]
    mod_parts = mod_parts.astype(jnp.float32).reshape(frame_count, 3, clip_count, -1)
    modulation = mod_parts[:, 0] + mod_parts[:, 1] + mod_parts[:, 2]
    modulation = modulation.transpose(1, 0, 2).reshape(clip_count, 2 * feat_width)
    shift_all, scale_all = modulation[:, :feat_width], modulation[:, feat_width:]
    shift_vec = lax.dynamic_index_in_dim(shift_all, clip_id, 0)
    scale_vec = lax.dynamic_index_in_dim(scale_all, clip_id, 0)

    def on_lanes(vector):
        return jnp.pad(vector, (0, lane - head_count)).reshape(1, lane)

    bias, fade_space, fade_time = on_lanes(step_bias), on_lanes(rate_space), on_lanes(rate_time)
    channel_head = jnp.arange(feat_width) // (feat_width // head_count)
    expand = (channel_head[None, :] == jnp.arange(lane)[:, None]).astype(jnp.bfloat16)
    collect = (channel_head[:, None] == jnp.arange(lane)[None, :]).astype(jnp.bfloat16)
    skip_full = jnp.repeat(skip_gain, feat_width // head_count).reshape(1, feat_width)
    normed, coeffs, logits, end_local, own_grad, end_decay = head(
        tokens, flat_grad, weights, step_w, shift_vec, scale_vec, bias, fade_space, expand
    )
    site_tokens, site_grad, state_in, later_grad = exchange_chain(
        tokens.reshape(frame_count, site_count, feat_width),
        flat_grad.reshape(frame_count, site_count, feat_width),
        end_local,
        own_grad,
        end_decay[0, :head_count],
    )
    mixed_part, pre_part, time_out, time_back, weight_grad = core(
        head_count,
        normed,
        flat_grad,
        coeffs,
        logits,
        state_in,
        later_grad,
        site_tokens.reshape(band_len, feat_width),
        site_grad.reshape(band_len, feat_width),
        weights,
        step_w,
        shift_all,
        scale_all,
        bias,
        fade_space,
        fade_time,
        skip_full,
        expand,
        collect,
    )
    frame_time, frame_back, weight_parts = back(
        time_out.reshape(frame_count, site_count, feat_width),
        time_back.reshape(frame_count, site_count, feat_width),
        weight_grad,
    )
    frame_time = frame_time.reshape(band_len, feat_width).astype(jnp.float32)
    mixed = (mixed_part + frame_time).astype(jnp.bfloat16)
    pre_grad = pre_part + frame_back.reshape(band_len, feat_width).astype(jnp.float32)
    tokens_wide = tokens.astype(jnp.float32)
    inverse = lax.rsqrt(jnp.mean(tokens_wide * tokens_wide, axis=-1, keepdims=True) + norm_eps)
    unit_rows = tokens_wide * inverse
    shift_grad = jnp.sum(pre_grad, axis=0)
    scale_grad = jnp.sum(pre_grad * unit_rows, axis=0)
    unit_grad = pre_grad * (1.0 + scale_vec)
    d_tokens = inverse * (unit_grad - unit_rows * jnp.mean(unit_grad * unit_rows, axis=-1, keepdims=True))

    band_sum = jnp.sum(weight_parts.astype(jnp.float32), axis=0).T.reshape(frame_count, -1)
    mod_term = jnp.concatenate([shift_grad, scale_grad]).reshape(frame_count, -1)
    payload = jnp.concatenate([band_sum, mod_term], axis=1)
    payload = jnp.pad(payload, ((0, 0), (0, -payload.shape[1] % (16 * lane))))
    arrived = plane(payload.reshape(frame_count, -1, lane).astype(jnp.bfloat16)).astype(jnp.float32)
    by_clip = jnp.sum(arrived.reshape(clip_count, clip_frames, *arrived.shape[1:]), axis=1)
    weight_sum = jnp.sum(by_clip, axis=0)
    mod_start = band_sum.shape[1]
    mod_width = mod_term.shape[1]
    mod_part = by_clip.reshape(clip_count, -1)[:, mod_start : mod_start + mod_width]
    mod_box = jnp.pad(mod_part, ((0, -clip_count % 8), (0, -mod_width % 128)))
    weight_box, mod_boxes = deliver(weight_sum, mod_box)
    weight_rows = weight_box.reshape(row_count, -1)[:, :mod_start].reshape(depth, -1) * factor
    grad_proj, grad_step = weight_rows[:, : 2 * state_size], weight_rows[:, 2 * state_size :]
    mod_sum = jnp.sum(mod_boxes, axis=0)[:clip_count, :mod_width]
    grad_mod = (
        jnp.dot(activated.astype(jnp.float32).T, mod_sum, precision=lax.Precision.HIGHEST) * factor
    )
    shape = cotangent.shape
    return (
        mixed.reshape(shape),
        d_tokens.astype(jnp.bfloat16).reshape(shape),
        grad_proj,
        grad_step,
        grad_mod,
    )


def solution(mesh):
    placed = (
        P("frame", "row", None, None),
        P("frame", "row", None, None),
        P(),
        P(None, "frame"),
        P("frame", None),
        P("frame", None),
        P(),
        P(),
        P(),
        P(),
    )
    return jax.shard_map(
        per_device,
        mesh=mesh,
        in_specs=placed,
        out_specs=(
            P("frame", "row", None, None),
            P("frame", "row", None, None),
            P("frame", None),
            P("frame", None),
            P(None, "frame"),
        ),
        check_vma=False,
    )
```

```python
import functools
import math

import jax
import jax.numpy as jnp
from jax import lax
from jax.experimental import pallas as pl
from jax.experimental.pallas import tpu as pltpu
from jax.sharding import PartitionSpec as P

norm_eps = 1e-05
MESH = pl.DeviceIdType.MESH
ANY = pl.BlockSpec(memory_space=pl.ANY)
VMEM = pl.BlockSpec(memory_space=pltpu.VMEM)
SMEM = pl.BlockSpec(memory_space=pltpu.SMEM)
CHAIN_CHUNKS = 16
CHAIN_LAG = 6
PLANE_WIDE = 4
CLIPS = 4
BIG = 56 * 2**20
PLANE_AHEAD = 8
PLANE_LATEST = 24


def at(frame=None, row=None):
    place = {}
    if frame is not None:
        place["frame"] = frame
    if row is not None:
        place["row"] = row
    return place


def tell(sem, **place):
    pl.semaphore_signal(sem, inc=1, device_id=at(**place), device_id_type=MESH)


def push(src, dst, send_sem, recv_sem, **place):
    return pltpu.make_async_remote_copy(
        src_ref=src,
        dst_ref=dst,
        send_sem=send_sem,
        recv_sem=recv_sem,
        device_id=at(**place),
        device_id_type=MESH,
    )


def each(start, stop, body):
    def step(k, carry):
        body(k)
        return carry

    lax.fori_loop(start, stop, step, 0)


def gather_kernel(src, out, y_send, y_recv, x_send, x_recv, c_send, c_recv, local_sem):
    high, wide = out.shape[0], out.shape[1]
    frame = lax.axis_index("frame")
    core, x, y = frame % 2, frame // 2 % wide, frame // (2 * wide)

    def index(y, x, core):
        return (y * wide + x) * 2 + core

    sibling = index(y, x, 1 - core)
    barrier = pltpu.get_barrier_semaphore()
    for k in range(1, high):
        tell(barrier, frame=index((y + k) % high, x, core))
    for k in range(1, wide):
        tell(barrier, frame=index(y, (x + k) % wide, core))
    tell(barrier, frame=sibling)
    own = pltpu.make_async_copy(src, out.at[y, x, core], local_sem)
    own.start()
    pl.semaphore_wait(barrier, high + wide - 1)

    def along_y(k, back=False):
        place = (y + high - k) % high if back else y
        peer = index((y + k) % high, x, core)
        return push(src, out.at[place, x, core], y_send.at[k], y_recv.at[k], frame=peer)

    def along_x(k, i, back=False):
        place = (y + high - k) % high
        held = src if k == 0 else out.at[place, x, core]
        column = (x + wide - i) % wide if back else x
        return push(
            held, out.at[place, column, core], x_send.at[k, i], x_recv.at[k, i],
            frame=index(y, (x + i) % wide, core),
        )

    def across(k, back=False):
        place = (y + high - k) % high
        side = 1 - core if back else core
        held = out.at[place, :, side]
        return push(out.at[place, :, core], held, c_send.at[k], c_recv.at[k], frame=sibling)

    near = sorted(range(1, high), key=lambda k: min(k, high - k))
    for k in near:
        along_y(k).start()
    for i in range(1, wide):
        along_x(0, i).start()
    for k in near:
        along_y(k, True).wait_recv()
        for i in range(1, wide):
            along_x(k, i).start()
    own.wait()
    for k in [0, *near]:
        for i in range(1, wide):
            along_x(k, i, True).wait_recv()
        across(k).start()
    for k in [0, *near]:
        across(k, True).wait_recv()
    for k in near:
        along_y(k).wait_send()
    for k in [0, *near]:
        for i in range(1, wide):
            along_x(k, i).wait_send()
        across(k).wait_send()


def gather(chunk):
    count = lax.axis_size("frame")
    wide = PLANE_WIDE
    high = count // (2 * wide)
    out = pl.pallas_call(
        gather_kernel,
        out_shape=jax.ShapeDtypeStruct((high, wide, 2, *chunk.shape), chunk.dtype),
        in_specs=[VMEM],
        out_specs=VMEM,
        scratch_shapes=[
            pltpu.SemaphoreType.DMA((high,)),
            pltpu.SemaphoreType.DMA((high,)),
            pltpu.SemaphoreType.DMA((high, wide)),
            pltpu.SemaphoreType.DMA((high, wide)),
            pltpu.SemaphoreType.DMA((high,)),
            pltpu.SemaphoreType.DMA((high,)),
            pltpu.SemaphoreType.DMA,
        ],
        compiler_params=pltpu.CompilerParams(collective_id=0, has_side_effects=True),
        name="gather",
    )(chunk)
    return out.reshape(count, *chunk.shape)


def plane_copies(frame, count, pairs, send, recv):
    def out_piece(i, k):
        peer = (frame + k) % count
        src, dst = pairs[i]
        return push(src.at[peer], dst.at[frame], send.at[i, k], recv.at[i, k], frame=peer)

    def in_piece(i, k):
        origin = (frame + count - k) % count
        src, dst = pairs[i]
        return push(src.at[origin], dst.at[origin], send.at[i, k], recv.at[i, k], frame=origin)

    return out_piece, in_piece


def plane_start(frame, count, pairs, send, recv, own_sem, some=None):
    out_piece, unused = plane_copies(frame, count, pairs, send, recv)
    for i, (src, dst) in enumerate(pairs):
        pltpu.make_async_copy(src.at[frame], dst.at[frame], own_sem.at[i]).start()

    def begin(k):
        for i in range(len(pairs)):
            out_piece(i, k).start()

    each(1, count if some is None else some, begin)
    return begin


def plane_wait(frame, count, pairs, send, recv, own_sem):
    out_piece, in_piece = plane_copies(frame, count, pairs, send, recv)

    def end(k):
        for i in range(len(pairs)):
            in_piece(i, k).wait_recv()
            out_piece(i, k).wait_send()

    each(1, count, end)
    for i, (src, dst) in enumerate(pairs):
        pltpu.make_async_copy(src.at[frame], dst.at[frame], own_sem.at[i]).wait()


def exchange_chain_kernel(
    per_head, xs, gs, end_local, own_grad, decay, rx, rg, state_in, later, fwd_out, bwd_out, send, recv, own_sem,
    fwd_send, fwd_recv, bwd_send, bwd_recv,
):
    frame, row = lax.axis_index("frame"), lax.axis_index("row")
    count, bands = lax.axis_size("frame"), lax.axis_size("row")
    height = end_local.shape[0] // CHAIN_CHUNKS
    barrier = pltpu.get_barrier_semaphore()
    each(1, count, lambda k: tell(barrier, frame=(frame + k) % count))

    @pl.when(row > 0)
    def _():
        tell(barrier, row=row - 1)

    @pl.when(row < bands - 1)
    def _():
        tell(barrier, row=row + 1)

    neighbours = jnp.where(row > 0, 1, 0) + jnp.where(row < bands - 1, 1, 0)
    pl.semaphore_wait(barrier, count - 1 + neighbours)

    def rows_of(c):
        return pl.ds(pl.multiple_of(c * height, height), height)

    def fwd(c):
        where = rows_of(c)
        return push(fwd_out.at[where], state_in.at[where], fwd_send.at[c], fwd_recv.at[c], row=row + 1)

    def bwd(c):
        where = rows_of(c)
        return push(bwd_out.at[where], later.at[where], bwd_send.at[c], bwd_recv.at[c], row=row - 1)

    def fwd_in(c):
        where = rows_of(c)
        return push(fwd_out.at[where], state_in.at[where], fwd_send.at[c], fwd_recv.at[c], row=row - 1)

    def bwd_in(c):
        where = rows_of(c)
        return push(bwd_out.at[where], later.at[where], bwd_send.at[c], bwd_recv.at[c], row=row + 1)

    def join(c, before, own, result):
        for j in range(height // per_head):
            where = pl.ds(pl.multiple_of(c * height + j * per_head, per_head), per_head)
            factor = decay[0, c * (height // per_head) + j]
            result[where, :] = (
                before[where, :].astype(jnp.float32) * factor + own[where, :]
            ).astype(result.dtype)

    @pl.when(row == 0)
    def _():
        state_in[...] = jnp.zeros_like(state_in)
        for c in range(CHAIN_CHUNKS):
            fwd_out[rows_of(c), :] = end_local[rows_of(c), :].astype(fwd_out.dtype)
            fwd(c).start()

    @pl.when(row == bands - 1)
    def _():
        later[...] = jnp.zeros_like(later)
        for c in range(CHAIN_CHUNKS):
            bwd_out[rows_of(c), :] = own_grad[rows_of(c), :].astype(bwd_out.dtype)
            bwd(c).start()

    slots = CHAIN_CHUNKS + (bands - 1) * CHAIN_LAG
    ahead = 1 + PLANE_AHEAD
    per_slot = -(-(count - ahead) // (slots - PLANE_LATEST))
    begin = plane_start(frame, count, [(xs, rx), (gs, rg)], send, recv, own_sem, ahead)

    def slot(s):
        f = s - row * CHAIN_LAG
        b = s - (bands - 1 - row) * CHAIN_LAG

        @pl.when(jnp.logical_and(row > 0, jnp.logical_and(f >= 0, f < CHAIN_CHUNKS)))
        def _():
            fwd_in(f).wait_recv()

            @pl.when(row < bands - 1)
            def _():
                join(f, state_in, end_local, fwd_out)
                fwd(f).start()

        @pl.when(jnp.logical_and(row < bands - 1, jnp.logical_and(b >= 0, b < CHAIN_CHUNKS)))
        def _():
            bwd_in(b).wait_recv()

            @pl.when(row > 0)
            def _():
                join(b, later, own_grad, bwd_out)
                bwd(b).start()

        first = jnp.minimum(ahead + s * per_slot, count)
        each(first, jnp.minimum(first + per_slot, count), begin)

    each(0, slots, slot)
    plane_wait(frame, count, [(xs, rx), (gs, rg)], send, recv, own_sem)

    @pl.when(row < bands - 1)
    def _():
        for c in range(CHAIN_CHUNKS):
            fwd(c).wait_send()

    @pl.when(row > 0)
    def _():
        for c in range(CHAIN_CHUNKS):
            bwd(c).wait_send()


def exchange_chain(per_head, xs, gs, end_local, own_grad, decay):
    count = lax.axis_size("frame")
    state = jax.ShapeDtypeStruct(end_local.shape, jnp.bfloat16)
    return pl.pallas_call(
        functools.partial(exchange_chain_kernel, per_head),
        out_shape=(
            jax.ShapeDtypeStruct(xs.shape, xs.dtype),
            jax.ShapeDtypeStruct(gs.shape, gs.dtype),
            state,
            state,
        ),
        in_specs=[ANY, ANY, VMEM, VMEM, SMEM],
        out_specs=(ANY, ANY, VMEM, VMEM),
        scratch_shapes=[
            pltpu.VMEM(end_local.shape, jnp.bfloat16),
            pltpu.VMEM(end_local.shape, jnp.bfloat16),
            pltpu.SemaphoreType.DMA((2, count)),
            pltpu.SemaphoreType.DMA((2, count)),
            pltpu.SemaphoreType.DMA((2,)),
            pltpu.SemaphoreType.DMA((CHAIN_CHUNKS,)),
            pltpu.SemaphoreType.DMA((CHAIN_CHUNKS,)),
            pltpu.SemaphoreType.DMA((CHAIN_CHUNKS,)),
            pltpu.SemaphoreType.DMA((CHAIN_CHUNKS,)),
        ],
        compiler_params=pltpu.CompilerParams(collective_id=1, has_side_effects=True),
        name="exchange_chain",
    )(xs, gs, end_local, own_grad, decay)


def finish_kernel(
    ts, bs, wp, ws, mixed_part, pre_part, tokens, scale,
    mixed_out, tokens_out, mod_out, weight_out,
    rt, rb, proj_parts, step_parts, pre, band, band_low, core_part, half, half_low, y_parts, x_parts, total,
    mod_src, a_parts, b_src, b_parts, z_src, z_parts,
    c_send, c_recv, y_send, y_recv, x_send, x_recv, d_send, d_recv, d_own,
    a_send, a_recv, b_send, b_recv, z_send, z_recv, t_send, t_recv, t_own, w_send, w_recv, w_own,
):
    frame, row = lax.axis_index("frame"), lax.axis_index("row")
    bands = lax.axis_size("row")
    length, width = pre.shape
    lanes = mod_src.shape[2]
    blocks = width // lanes
    wide, high = x_parts.shape[0], y_parts.shape[0]
    tall = total.shape[0]
    core, x, y = frame % 2, frame // 2 % wide, frame // (2 * wide)
    side = half.shape[0]
    coef = proj_parts.shape[2]

    def index(y, x, core):
        return (y * wide + x) * 2 + core

    sibling = index(y, x, 1 - core)
    per_home = 2
    home = row * high + core * (high // 2) + y // per_home
    piece = y % per_home
    from_row, from_core, from_x = frame // high, frame % high // (high // 2), row // per_home

    def source(i):
        return index(frame % (high // 2) * per_home + i, from_x, from_core)

    def other(f, r):
        return jnp.logical_or(f != frame, r != row)

    group = 2 * wide
    own = x * 2 + core

    def mate(k):
        return y * group + (own + k) % group

    barrier = pltpu.get_barrier_semaphore()
    count = lax.axis_size("frame")
    each(1, count, lambda k: tell(barrier, frame=(frame + k) % count))
    each(1, bands, lambda k: tell(barrier, row=(row + k) % bands))
    for i in range(per_home):

        @pl.when(other(source(i), from_row))
        def _():
            tell(barrier, frame=source(i), row=from_row)

    local = jnp.where(home == frame, jnp.where(row // per_home == x, 1, 0), 0)

    squares = jnp.zeros((length, lanes), jnp.float32)
    for j in range(blocks):
        where = slice(j * lanes, (j + 1) * lanes)
        squares += tokens[:, where].astype(jnp.float32) ** 2
    inverse = lax.rsqrt(jnp.sum(squares, axis=1, keepdims=True) * (1.0 / width) + norm_eps)
    pl.semaphore_wait(barrier, count - 1 + bands - 1 + per_home - local)

    def rows_at(k, size):
        return pl.ds(pl.multiple_of(k * size, size), size)

    share = band.shape[0]

    def pieces(j):
        return (wp.at[rows_at(j, share), :], proj_parts), (ws.at[:, rows_at(j, share)], step_parts)

    def w_out(i, k):
        peer = (row + k) % bands
        src, dst = pieces(peer)[i]
        return push(src, dst.at[row], w_send.at[i, k], w_recv.at[i, k], row=peer)

    def w_in(i, k):
        origin = (row + bands - k) % bands
        src, dst = pieces(origin)[i]
        return push(src, dst.at[origin], w_send.at[i, k], w_recv.at[i, k], row=origin)

    def w_self(i):
        src, dst = pieces(row)[i]
        return pltpu.make_async_copy(src, dst.at[row], w_own.at[i])

    def w_begin(k):
        for i in range(2):
            w_out(i, k).start()

    def w_end(k):
        for i in range(2):
            w_in(i, k).wait_recv()
            w_out(i, k).wait_send()

    for i in range(2):
        w_self(i).start()
    each(1, bands, w_begin)
    plane_start(frame, count, [(bs, rb), (ts, rt)], t_send, t_recv, t_own)
    each(1, bands, w_end)
    for i in range(2):
        w_self(i).wait()

    step = 2 * tall
    for i in range(band.shape[0] // step):
        rows = slice(i * step, (i + 1) * step)
        part = proj_parts[0, rows, :].astype(jnp.float32)
        for j in range(1, proj_parts.shape[0]):
            part += proj_parts[j, rows, :].astype(jnp.float32)
        band[rows, :coef] = part
    part = step_parts[0].astype(jnp.float32)
    for j in range(1, step_parts.shape[0]):
        part += step_parts[j].astype(jnp.float32)
    filled = jnp.concatenate([part, jnp.zeros((lanes - part.shape[0], part.shape[1]), jnp.float32)], axis=0)
    band[:, coef:] = filled.T
    band_low[...] = band[...].astype(band_low.dtype)
    across = push(band_low.at[rows_at(1 - core, side), :], core_part, c_send, c_recv, frame=sibling)
    across.start()

    across.wait_recv()
    half[...] = band[rows_at(core, side), :] + core_part[...].astype(jnp.float32)
    half_low[...] = half[...].astype(half_low.dtype)

    def y_out(k):
        peer = (y + k) % high
        return push(
            half_low.at[rows_at(peer, tall), :], y_parts.at[y], y_send.at[k], y_recv.at[k],
            frame=index(peer, x, core),
        )

    def y_in(k):
        origin = (y + high - k) % high
        return push(
            half_low.at[rows_at(0, tall), :], y_parts.at[origin], y_send.at[k], y_recv.at[k],
            frame=index(origin, x, core),
        )

    for k in range(1, high):
        y_out(k).start()
    y_parts[pl.ds(y, 1)] = half_low[rows_at(y, tall), :][None]

    for k in range(1, high):
        y_in(k).wait_recv()
    x_parts[pl.ds(x, 1)] = jnp.sum(y_parts[...].astype(jnp.float32), axis=0)[None]

    def x_out(k):
        return push(
            x_parts.at[x], x_parts.at[x], x_send.at[k], x_recv.at[k], frame=index(y, (x + k) % wide, core)
        )

    def x_in(k):
        origin = (x + wide - k) % wide
        return push(
            x_parts.at[origin], x_parts.at[origin], x_send.at[k], x_recv.at[k], frame=index(y, origin, core)
        )

    for k in range(1, wide):
        x_out(k).start()
    for k in range(1, wide):
        x_in(k).wait_recv()
    total[...] = jnp.sum(x_parts[...], axis=0)

    def d_out(i):
        return push(total, weight_out.at[piece], d_send.at[i], d_recv.at[piece], frame=home, row=x * per_home + i)

    def d_in(i):
        return push(total, weight_out.at[i], d_send.at[0], d_recv.at[i], frame=source(i), row=from_row)

    d_self = pltpu.make_async_copy(total, weight_out.at[piece], d_own)
    for i in range(per_home):
        away = other(home, x * per_home + i)

        @pl.when(away)
        def _():
            d_out(i).start()

        @pl.when(jnp.logical_not(away))
        def _():
            d_self.start()

    plane_wait(frame, count, [(bs, rb), (ts, rt)], t_send, t_recv, t_own)

    along = jnp.zeros((length, lanes), jnp.float32)
    for j in range(blocks):
        where = slice(j * lanes, (j + 1) * lanes)
        value = pre_part[:, where] + read(rb, where).astype(jnp.float32)
        pre[:, where] = value
        matched = value * (tokens[:, where].astype(jnp.float32) * inverse)
        to_y, to_x = j // wide, j % wide
        mod_src[to_x, to_y : to_y + 1, :] = jnp.sum(value, axis=0, keepdims=True)
        to_y += blocks // wide
        mod_src[to_x, to_y : to_y + 1, :] = jnp.sum(matched, axis=0, keepdims=True)
        along += matched * (1.0 + scale[:, where])

    def a_out(k):
        peer = (own + k) % group
        return push(mod_src.at[peer // 2], a_parts.at[own], a_send.at[k], a_recv.at[k], frame=mate(k))

    def a_in(k):
        origin = (own + group - k) % group
        return push(mod_src.at[0], a_parts.at[origin], a_send.at[k], a_recv.at[k], frame=mate(k))

    for k in range(1, group):
        a_out(k).start()
    a_parts[pl.ds(own, 1)] = mod_src[pl.ds(x, 1)]
    along = jnp.sum(along, axis=1, keepdims=True) * (1.0 / width)
    for j in range(blocks):
        where = slice(j * lanes, (j + 1) * lanes)
        unit = tokens[:, where].astype(jnp.float32) * inverse
        pulled = pre[:, where] * (1.0 + scale[:, where])
        tokens_out[:, where] = (inverse * (pulled - unit * along)).astype(tokens_out.dtype)
        mixed_out[:, where] = (mixed_part[:, where] + read(rt, where).astype(jnp.float32)).astype(
            mixed_out.dtype
        )

    for k in range(1, group):
        a_in(k).wait_recv()
    b_src[...] = jnp.sum(a_parts[...], axis=0)

    def b_out(k):
        return push(
            b_src, b_parts.at[y], b_send.at[k], b_recv.at[k], frame=index((y + k) % high, x, core)
        )

    def b_in(k):
        origin = (y + high - k) % high
        return push(b_src, b_parts.at[origin], b_send.at[k], b_recv.at[k], frame=index(origin, x, core))

    for k in range(1, high):
        b_out(k).start()
    b_parts[pl.ds(y, 1)] = b_src[...][None]
    for k in range(1, high):
        b_in(k).wait_recv()
    z_src[...] = jnp.zeros_like(z_src)
    per_clip = high // CLIPS
    for c in range(CLIPS):
        chosen = b_parts[c * per_clip, pl.ds(y, 1), :]
        for i in range(1, per_clip):
            chosen += b_parts[c * per_clip + i, pl.ds(y, 1), :]
        z_src[c : c + 1, :] = chosen

    def z_out(k):
        return push(z_src, z_parts.at[row], z_send.at[k], z_recv.at[k], row=(row + k) % bands)

    def z_in(k):
        origin = (row + bands - k) % bands
        return push(z_src, z_parts.at[origin], z_send.at[k], z_recv.at[k], row=origin)

    for k in range(1, z_parts.shape[0]):
        z_out(k).start()
    z_parts[pl.ds(row, 1)] = z_src[...][None]
    for k in range(1, z_parts.shape[0]):
        z_in(k).wait_recv()
    mod_out[...] = jnp.sum(z_parts[...], axis=0)
    for i in range(per_home):
        came = other(source(i), from_row)

        @pl.when(came)
        def _():
            d_in(i).wait_recv()

        @pl.when(jnp.logical_not(came))
        def _():
            d_self.wait()

    across.wait_send()
    for k in range(1, group):
        a_out(k).wait_send()
    for k in range(1, high):
        y_out(k).wait_send()
        b_out(k).wait_send()
    for k in range(1, wide):
        x_out(k).wait_send()
    for k in range(1, z_parts.shape[0]):
        z_out(k).wait_send()
    for i in range(per_home):

        @pl.when(other(home, x * per_home + i))
        def _():
            d_out(i).wait_send()


def finish(ts, bs, wp, ws, mixed_part, pre_part, tokens, scale):
    count, bands = lax.axis_size("frame"), lax.axis_size("row")
    length, width = tokens.shape
    lanes = 128
    wide = PLANE_WIDE
    high = count // (2 * wide)
    share, coef = width // bands, wp.shape[1] + lanes
    tall = share // 2 // high
    low = jax.ShapeDtypeStruct(tokens.shape, tokens.dtype)
    f32, bf16 = jnp.float32, jnp.bfloat16
    sems = pltpu.SemaphoreType.DMA
    return pl.pallas_call(
        finish_kernel,
        out_shape=(
            low,
            low,
            jax.ShapeDtypeStruct((8, lanes), f32),
            jax.ShapeDtypeStruct((2, tall, coef), f32),
        ),
        in_specs=[VMEM] * 8,
        out_specs=(VMEM,) * 4,
        scratch_shapes=[
            pltpu.VMEM(ts.shape, bf16),
            pltpu.VMEM(bs.shape, bf16),
            pltpu.VMEM((bands, share, wp.shape[1]), bf16),
            pltpu.VMEM((bands, ws.shape[0], share), bf16),
            pltpu.VMEM((length, width), f32),
            pltpu.VMEM((share, coef), f32),
            pltpu.VMEM((share, coef), bf16),
            pltpu.VMEM((share // 2, coef), bf16),
            pltpu.VMEM((share // 2, coef), f32),
            pltpu.VMEM((share // 2, coef), bf16),
            pltpu.VMEM((high, tall, coef), bf16),
            pltpu.VMEM((wide, tall, coef), f32),
            pltpu.VMEM((tall, coef), f32),
            pltpu.VMEM((wide, high, lanes), f32),
            pltpu.VMEM((2 * wide, high, lanes), f32),
            pltpu.VMEM((high, lanes), f32),
            pltpu.VMEM((high, high, lanes), f32),
            pltpu.VMEM((8, lanes), f32),
            pltpu.VMEM((bands, 8, lanes), f32),
            sems,
            sems,
            sems((high,)),
            sems((high,)),
            sems((wide,)),
            sems((wide,)),
            sems((2,)),
            sems((2,)),
            sems,
            sems((2 * wide,)),
            sems((2 * wide,)),
            sems((high,)),
            sems((high,)),
            sems((bands,)),
            sems((bands,)),
            sems((2, count)),
            sems((2, count)),
            sems((2,)),
            sems((2, bands)),
            sems((2, bands)),
            sems((2,)),
        ],
        compiler_params=pltpu.CompilerParams(collective_id=3, has_side_effects=True, vmem_limit_bytes=BIG),
        name="finish",
    )(ts, bs, wp, ws, mixed_part, pre_part, tokens, scale)


def time_embed(timestep, embed_dim):
    half_dim = embed_dim // 2
    frequency = jnp.exp(-math.log(10000.0) * jnp.arange(half_dim, dtype=jnp.float32) / half_dim)
    angles = timestep.astype(jnp.float32)[:, None] * frequency[None, :]
    return jax.nn.silu(jnp.concatenate([jnp.cos(angles), jnp.sin(angles)], axis=1))


def halves(values):
    high = values.astype(jnp.bfloat16)
    return high, (values - high.astype(jnp.float32)).astype(jnp.bfloat16)


def mm(a, b):
    return jnp.dot(a, b, preferred_element_type=jnp.float32)


def mm_nt(a, b):
    return lax.dot_general(a, b, (((1,), (1,)), ((), ())), preferred_element_type=jnp.float32)


def mm_tn(a, b):
    return lax.dot_general(a, b, (((0,), (0,)), ((), ())), preferred_element_type=jnp.float32)


def with_ones(ones, values, dot):
    first = values.astype(jnp.bfloat16)
    rest = values - first.astype(jnp.float32)
    second = rest.astype(jnp.bfloat16)
    third = (rest - second.astype(jnp.float32)).astype(jnp.bfloat16)
    return dot(ones, first) + dot(ones, second) + dot(ones, third)


def earlier_mask(length, sites):
    t = lax.broadcasted_iota(jnp.int32, (length, length), 0)
    u = lax.broadcasted_iota(jnp.int32, (length, length), 1)
    return jnp.logical_and(u <= t, lax.rem(t, sites) == lax.rem(u, sites))


def steps_of(logits, bias, rate, mask):
    raised = logits.astype(jnp.float32) + bias
    step = jnp.maximum(raised, 0.0) + jnp.log1p(jnp.exp(-jnp.abs(raised)))
    lower = jnp.where(mask, 1.0, 0.0).astype(jnp.bfloat16)
    return raised, step, with_ones(lower, -step * rate, mm)


def stacked(values):
    parts = [halves(v) for v in values]
    return jnp.concatenate([p[0] for p in parts] + [p[1] for p in parts], axis=0)


def split_sum(product, sizes):
    total = sum(sizes)
    result, start = [], 0
    for size in sizes:
        result.append(product[start : start + size] + product[total + start : total + start + size])
        start += size
    return result


def spread(columns, expand, where):
    length = columns.shape[0]
    return split_sum(mm(columns, expand[:, where]), [length // 2])[0]


def per_head(values, expand, where):
    return split_sum(mm_nt(stacked(values), expand[:, where]), [v.shape[0] for v in values])


def head_kernel(
    tokens, grad, weights, step_w, shift, scale, small, expand,
    normed_out, coeff_out, logit_out, end_out, own_out, decay_out,
):
    length, width = tokens.shape
    lanes = step_w.shape[1]
    values = tokens[...].astype(jnp.float32)
    inverse = lax.rsqrt(jnp.mean(values * values, axis=1, keepdims=True) + norm_eps)
    normed_out[...] = (values * inverse * (1.0 + scale[...]) + shift[...]).astype(jnp.bfloat16)
    project(normed_out, weights, step_w, coeff_out, logit_out)
    b_part, c_part = coeff_out[:, :lanes], coeff_out[:, lanes:]
    mask = earlier_mask(length, 1)
    unused, step, log = steps_of(logit_out[...], small[0:1, :], small[1:2, :], mask)
    last = log[length - 1 :, :]
    decay_out[...] = jnp.exp(last)
    lead = jnp.exp(last - log) * step
    reach = jnp.exp(log) * (1.0 / lanes)
    columns = stacked([lead, reach])
    for j in range(width // lanes):
        where = slice(j * lanes, (j + 1) * lanes)
        wide = spread(columns, expand, where)
        scaled = (normed_out[:, where].astype(jnp.float32) * wide[:length]).astype(jnp.bfloat16)
        end_out[where, :] = mm_tn(scaled, b_part)
        pulled = (grad[:, where].astype(jnp.float32) * wide[length:]).astype(jnp.bfloat16)
        own_out[where, :] = mm_tn(pulled, c_part)


def project(normed, weights, step_w, coeff_out, logit_out):
    lanes = step_w.shape[1]
    count = weights.shape[0]
    depth = normed.shape[1] // count
    for i in range(2):
        w = weights[:, i * depth : (i + 1) * depth, :].reshape(count * depth, lanes)
        coeff_out[:, i * lanes : (i + 1) * lanes] = mm(normed[...], w).astype(jnp.bfloat16)
    logit_out[...] = mm(normed[...], step_w[...]).astype(jnp.bfloat16)


def read(ref, where):
    if len(ref.shape) == 2:
        return ref[:, where]
    values = ref[:, :, where]
    return values.reshape(ref.shape[0] * ref.shape[1], values.shape[2])


def write(ref, where, values):
    values = values.astype(ref.dtype)
    if len(ref.shape) == 2:
        ref[:, where] = values
    else:
        ref[:, :, where] = values.reshape(*ref.shape[:2], values.shape[1])


def scan_pass(
    x_ref, g_ref, coeffs, logits, bias, rate, weights, step_w, expand, skip, state, later,
    mixed_ref, dx_ref, back_ref, wp_ref, ws_ref, sites, first,
):
    length, width = x_ref.shape
    lanes = coeffs.shape[1] // 2
    space = state is not None
    b_part, c_part = coeffs[:, :lanes], coeffs[:, lanes:]
    mask = earlier_mask(length, sites)
    raised, step, log = steps_of(logits[...], bias, rate, mask)
    log_t = log.T
    scores = jnp.where(mask, mm_nt(c_part, b_part) * (1.0 / lanes), 0.0)
    left = lax.broadcasted_iota(jnp.int32, (length, lanes), 1) < lanes // 2
    d_scores = jnp.zeros((length, length), jnp.float32)
    pull_out = jnp.zeros((length, lanes), jnp.float32)
    pull_in = jnp.zeros((length, lanes), jnp.float32)
    d_b = jnp.zeros((length, lanes), jnp.float32)
    d_c = jnp.zeros((length, lanes), jnp.float32)
    if space:
        last = log[length - 1 :, :]
        reach_all = jnp.exp(log) * (1.0 / lanes)
        fade_all = jnp.exp(last - log)
        d_last = jnp.zeros((16, lanes), jnp.float32)
        state_rows = []
        columns = stacked([step, reach_all, fade_all, skip])
    else:
        columns = stacked([step])
    for j in range(width // lanes):
        where = slice(j * lanes, (j + 1) * lanes)
        x, g = read(x_ref, where), read(g_ref, where)
        wide_x, wide_g = x.astype(jnp.float32), g.astype(jnp.float32)
        spread_all = spread(columns, expand, where)
        step_x = spread_all[:length]
        stepped_wide = wide_x * step_x
        stepped = stepped_wide.astype(jnp.bfloat16)
        falls = []
        for h in (2 * j, 2 * j + 1):
            falls.append(jnp.exp(jnp.minimum(log[:, h : h + 1] - log_t[h : h + 1, :], 0.0)))
        pair = [(scores * fall).astype(jnp.bfloat16) for fall in falls]
        outs = mm(jnp.concatenate(pair, axis=0), stepped)
        backs = mm_tn(jnp.concatenate(pair, axis=1), g)
        left_g = jnp.where(left, wide_g, 0.0).astype(jnp.bfloat16)
        right_g = jnp.where(left, 0.0, wide_g).astype(jnp.bfloat16)
        d_pair = mm_nt(jnp.concatenate([left_g, right_g], axis=0), stepped)
        d_scores += d_pair[:length] * falls[0] + d_pair[length:] * falls[1]
        out = jnp.where(left, outs[:length], outs[length:])
        d_step_x = jnp.where(left, backs[:length], backs[length:])
        if space:
            held, late = state[where, :], later[where, :]
            reach, fade = spread_all[length : 2 * length], spread_all[2 * length : 3 * length]
            gain = spread_all[3 * length : 3 * length + 1]
            out += mm_nt(c_part, held) * reach
            d_c += mm((wide_g * reach).astype(jnp.bfloat16), held)
            from_end = mm_nt(b_part, late) * fade
            d_step_x += from_end
            d_b += mm((stepped_wide * fade).astype(jnp.bfloat16), late)
            to_last = jnp.sum(stepped_wide * from_end, axis=0, keepdims=True)
            both = held.astype(jnp.float32) * late.astype(jnp.float32)
            half = lanes // 2
            state_rows += [
                jnp.sum(both[:half], axis=0, keepdims=True),
                jnp.sum(both[half:], axis=0, keepdims=True),
            ]
            mixed_ref[:, where] = out + gain * wide_x
            direct = (wide_g * gain).astype(jnp.bfloat16).astype(jnp.float32)
            dx_ref[:, where] = step_x * d_step_x + direct
        else:
            write(mixed_ref, where, out)
            dx_ref[:, where] = step_x * d_step_x
        sums = [wide_g * out, wide_x * d_step_x]
        if space:
            sums.append(jnp.broadcast_to(to_last, (16, lanes)))
        sums = per_head(sums, expand, where)
        pull_out += sums[0]
        pull_in += sums[1]
        if space:
            d_last += sums[2]
    d_low = (jnp.where(mask, d_scores, 0.0) * (1.0 / lanes)).astype(jnp.bfloat16)
    d_c += mm(d_low, b_part)
    d_b += mm_tn(d_low, c_part)
    d_log = pull_out - step * pull_in
    if space:
        states = jnp.concatenate([*state_rows, jnp.zeros((lanes - len(state_rows), lanes), jnp.float32)], axis=0)
        high, low = halves(states)
        ones = jnp.ones((16, lanes), jnp.bfloat16)
        d_last += (mm_nt(ones, high) + mm_nt(ones, low)) * jnp.exp(last)
        at_end = lax.broadcasted_iota(jnp.int32, (length, lanes), 0) == length - 1
        d_log += jnp.where(at_end, d_last[:1, :], 0.0)
    lower = jnp.where(mask, 1.0, 0.0).astype(jnp.bfloat16)
    d_fall = with_ones(lower, d_log, mm_tn)
    d_step = pull_in - rate * d_fall
    d_logit = (d_step * jax.nn.sigmoid(raised)).astype(jnp.bfloat16)
    low_b, low_c = d_b.astype(jnp.bfloat16), d_c.astype(jnp.bfloat16)
    count = weights.shape[0]
    depth = width // count
    block = 8
    for k in range(count // block):
        cols = slice(k * block * depth, (k + 1) * block * depth)
        w_b = weights[k * block : (k + 1) * block, :depth, :].reshape(block * depth, lanes)
        w_c = weights[k * block : (k + 1) * block, depth : 2 * depth, :].reshape(block * depth, lanes)
        total = (
            dx_ref[:, cols] + mm_nt(low_b, w_b) + mm_nt(low_c, w_c) + mm_nt(d_logit, step_w[cols, :])
        )
        write(back_ref, cols, total)
        x = x_ref[:, cols]
        terms = ((wp_ref, cols, slice(0, lanes), mm_tn(x, low_b)), (wp_ref, cols, slice(lanes, None), mm_tn(x, low_c)))
        terms += ((ws_ref, slice(None), cols, mm_tn(d_logit, x)[: ws_ref.shape[0]]),)
        for ref, rows, columns, term in terms:
            ref[rows, columns] = term if first else ref[rows, columns] + term


def core_kernel(
    normed, grad, coeffs, logits, state, later, site_tokens, site_grad, weights, step_w, shift_all, scale_all,
    small, expand,
    mixed_out, pre_out, time_out, back_out, wp_out, ws_out, site_normed, site_coeffs, site_logits, dx, wp, ws,
):
    length, width = normed.shape
    bias, rate_space, rate_time = (small[i : i + 1, :] for i in range(3))
    skip = jnp.broadcast_to(small[3:4, :], (16, small.shape[1]))
    clips = shift_all.shape[0]
    sites = length // weights.shape[0]
    part = length // clips
    for c in range(clips):
        rows = slice(c * part, (c + 1) * part)
        frames = slice(c * part // sites, (c + 1) * part // sites)
        values = site_tokens[frames].reshape(part, width).astype(jnp.float32)
        inverse = lax.rsqrt(jnp.mean(values * values, axis=1, keepdims=True) + norm_eps)
        site_normed[rows, :] = (
            values * inverse * (1.0 + scale_all[c : c + 1, :]) + shift_all[c : c + 1, :]
        ).astype(jnp.bfloat16)
    project(site_normed, weights, step_w, site_coeffs, site_logits)
    scan_pass(
        site_normed, site_grad, site_coeffs, site_logits, bias, rate_time, weights, step_w, expand,
        None, None, None, time_out, dx, back_out, wp, ws, sites, True,
    )
    scan_pass(
        normed, grad, coeffs, logits, bias, rate_space, weights, step_w, expand,
        skip, state, later, mixed_out, dx, pre_out, wp, ws, 1, False,
    )
    wp_out[...] = wp[...].astype(jnp.bfloat16)
    ws_out[...] = ws[...].astype(jnp.bfloat16)


def head(tokens, grad, weights, step_w, shift, scale, small, expand):
    length, width = tokens.shape
    lanes = step_w.shape[1]
    low = functools.partial(jax.ShapeDtypeStruct, dtype=jnp.bfloat16)
    wide = functools.partial(jax.ShapeDtypeStruct, dtype=jnp.float32)
    return pl.pallas_call(
        head_kernel,
        out_shape=(
            low((length, width)),
            low((length, 2 * lanes)),
            low((length, lanes)),
            wide((width, lanes)),
            wide((width, lanes)),
            wide((1, lanes)),
        ),
        in_specs=[VMEM] * 8,
        out_specs=(VMEM,) * 6,
        compiler_params=pltpu.CompilerParams(vmem_limit_bytes=BIG),
        name="head",
    )(tokens, grad, weights, step_w, shift, scale, small, expand)


def core(heads, *operands):
    normed, coeffs, weights = operands[0], operands[2], operands[8]
    length, width = normed.shape
    lanes = coeffs.shape[1] // 2
    low = functools.partial(jax.ShapeDtypeStruct, dtype=jnp.bfloat16)
    wide = functools.partial(jax.ShapeDtypeStruct, dtype=jnp.float32)
    return pl.pallas_call(
        core_kernel,
        out_shape=(
            wide((length, width)),
            wide((length, width)),
            low(operands[6].shape),
            low(operands[6].shape),
            low((width, 2 * lanes)),
            low((heads, width)),
        ),
        in_specs=[VMEM] * 14,
        out_specs=(VMEM,) * 6,
        scratch_shapes=[
            pltpu.VMEM((length, width), jnp.bfloat16),
            pltpu.VMEM((length, 2 * lanes), jnp.bfloat16),
            pltpu.VMEM((length, lanes), jnp.bfloat16),
            pltpu.VMEM((length, width), jnp.float32),
            pltpu.VMEM((width, 2 * lanes), jnp.float32),
            pltpu.VMEM((heads, width), jnp.float32),
        ],
        compiler_params=pltpu.CompilerParams(vmem_limit_bytes=BIG),
        name="core",
    )(*operands)


def three_parts(values):
    first = lax.reduce_precision(values, 8, 7)
    second = lax.reduce_precision(values - first, 8, 7)
    return first, second, values - first - second


def per_device(
    tokens,
    cotangent,
    timestep,
    mod_weight,
    proj_weight,
    step_weight,
    step_bias,
    rate_space,
    rate_time,
    skip_gain,
):
    frame_count = lax.axis_size("frame")
    row_count = lax.axis_size("row")
    frame_id = lax.axis_index("frame")
    feat_width = tokens.shape[-1]
    band_len = tokens.shape[1] * tokens.shape[2]
    clip_count = timestep.shape[0]
    clip_frames = frame_count // clip_count
    site_count = band_len // frame_count
    head_count = rate_space.shape[0]
    state_size = proj_weight.shape[1] // 2
    depth = proj_weight.shape[0]
    clip_id = frame_id // clip_frames
    factor = (frame_count * row_count * band_len) ** (-0.5)
    tokens = tokens.reshape(band_len, feat_width)
    flat_grad = cotangent.reshape(band_len, feat_width)

    activated = time_embed(timestep, mod_weight.shape[0]).astype(jnp.bfloat16)
    mod_cols = jnp.dot(activated, mod_weight, preferred_element_type=jnp.float32)
    lane = state_size
    mod_rows = [part.reshape(-1, lane).astype(jnp.bfloat16) for part in three_parts(mod_cols)]
    rows = [proj_weight[:, :state_size], proj_weight[:, state_size:], step_weight.reshape(-1, lane), *mod_rows]
    used = sum(r.shape[0] for r in rows)
    chunk = jnp.concatenate([*rows, jnp.zeros((-used % 16, lane), jnp.bfloat16)], axis=0)
    gathered = gather(chunk)
    step_rows = depth * head_count // lane
    step_full = gathered[:, 2 * depth : 2 * depth + step_rows].reshape(feat_width, head_count)
    step_w = jnp.pad(step_full, ((0, 0), (0, lane - head_count)))
    mod_height = mod_rows[0].shape[0]
    mod_parts = gathered[:, 2 * depth + step_rows : 2 * depth + step_rows + 3 * mod_height]
    mod_parts = mod_parts.astype(jnp.float32).reshape(frame_count, 3, clip_count, -1)
    modulation = mod_parts[:, 0] + mod_parts[:, 1] + mod_parts[:, 2]
    modulation = modulation.transpose(1, 0, 2).reshape(clip_count, 2 * feat_width)
    shift_all, scale_all = modulation[:, :feat_width], modulation[:, feat_width:]
    shift_vec = lax.dynamic_index_in_dim(shift_all, clip_id, 0)
    scale_vec = lax.dynamic_index_in_dim(scale_all, clip_id, 0)

    small = jnp.pad(jnp.stack([step_bias, rate_space, rate_time, skip_gain]), ((0, 4), (0, lane - head_count)))
    channel_head = jnp.arange(feat_width) // (feat_width // head_count)
    expand = (channel_head[None, :] == jnp.arange(lane)[:, None]).astype(jnp.bfloat16)
    normed, coeffs, logits, end_local, own_grad, end_decay = head(
        tokens, flat_grad, gathered, step_w, shift_vec, scale_vec, small, expand
    )
    site_tokens, site_grad, state_in, later_grad = exchange_chain(
        feat_width // head_count,
        tokens.reshape(frame_count, site_count, feat_width),
        flat_grad.reshape(frame_count, site_count, feat_width),
        end_local,
        own_grad,
        end_decay,
    )
    mixed_part, pre_part, time_out, time_back, proj_grad, step_grad = core(
        head_count,
        normed,
        flat_grad,
        coeffs,
        logits,
        state_in,
        later_grad,
        site_tokens,
        site_grad,
        gathered,
        step_w,
        shift_all,
        scale_all,
        small,
        expand,
    )
    mixed, d_tokens, mod_sum, weight_sum = finish(
        time_out,
        time_back,
        proj_grad,
        step_grad,
        mixed_part,
        pre_part,
        tokens,
        scale_vec,
    )
    weight_rows = weight_sum.reshape(depth, -1) * factor
    grad_proj = weight_rows[:, : 2 * state_size]
    grad_step = weight_rows[:, 2 * state_size : 2 * state_size + head_count]
    mod_width = mod_weight.shape[1]
    mod_half = lax.dynamic_slice_in_dim(mod_sum[:clip_count], frame_id % 2 * mod_width, mod_width, axis=1)
    grad_mod = (
        jnp.dot(activated.astype(jnp.float32).T, mod_half, precision=lax.Precision.HIGHEST) * factor
    )
    shape = cotangent.shape
    return (
        mixed.reshape(shape),
        d_tokens.reshape(shape),
        grad_proj,
        grad_step,
        grad_mod,
    )


def solution(mesh):
    placed = (
        P("frame", "row", None, None),
        P("frame", "row", None, None),
        P(),
        P(None, "frame"),
        P("frame", None),
        P("frame", None),
        P(),
        P(),
        P(),
        P(),
    )
    return jax.shard_map(
        per_device,
        mesh=mesh,
        in_specs=placed,
        out_specs=(
            P("frame", "row", None, None),
            P("frame", "row", None, None),
            P("frame", None),
            P("frame", None),
            P(None, "frame"),
        ),
        check_vma=False,
    )
```

```python
import functools
import math

import jax
import jax.numpy as jnp
from jax import lax
from jax.experimental import pallas as pl
from jax.experimental.pallas import tpu as pltpu
from jax.sharding import PartitionSpec as P

norm_eps = 1e-05
MESH = pl.DeviceIdType.MESH
ANY = pl.BlockSpec(memory_space=pl.ANY)
VMEM = pl.BlockSpec(memory_space=pltpu.VMEM)
SMEM = pl.BlockSpec(memory_space=pltpu.SMEM)
CHAIN_CHUNKS = 16
CHAIN_LAG = 6
PLANE_WIDE = 4
CLIPS = 4
BIG = 56 * 2**20
PLANE_AHEAD = 8
PLANE_LATEST = 24


def at(frame=None, row=None):
    place = {}
    if frame is not None:
        place["frame"] = frame
    if row is not None:
        place["row"] = row
    return place


def tell(sem, **place):
    pl.semaphore_signal(sem, inc=1, device_id=at(**place), device_id_type=MESH)


def push(src, dst, send_sem, recv_sem, **place):
    return pltpu.make_async_remote_copy(
        src_ref=src,
        dst_ref=dst,
        send_sem=send_sem,
        recv_sem=recv_sem,
        device_id=at(**place),
        device_id_type=MESH,
    )


def each(start, stop, body):
    def step(k, carry):
        body(k)
        return carry

    lax.fori_loop(start, stop, step, 0)


def gather_kernel(src, out, y_send, y_recv, x_send, x_recv, c_send, c_recv, local_sem):
    high, wide = out.shape[0], out.shape[1]
    frame = lax.axis_index("frame")
    core, x, y = frame % 2, frame // 2 % wide, frame // (2 * wide)

    def index(y, x, core):
        return (y * wide + x) * 2 + core

    sibling = index(y, x, 1 - core)
    barrier = pltpu.get_barrier_semaphore()
    for k in range(1, high):
        tell(barrier, frame=index((y + k) % high, x, core))
    for k in range(1, wide):
        tell(barrier, frame=index(y, (x + k) % wide, core))
    tell(barrier, frame=sibling)
    own = pltpu.make_async_copy(src, out.at[y, x, core], local_sem)
    own.start()
    pl.semaphore_wait(barrier, high + wide - 1)

    def along_y(k, back=False):
        place = (y + high - k) % high if back else y
        peer = index((y + k) % high, x, core)
        return push(src, out.at[place, x, core], y_send.at[k], y_recv.at[k], frame=peer)

    def along_x(k, i, back=False):
        place = (y + high - k) % high
        held = src if k == 0 else out.at[place, x, core]
        column = (x + wide - i) % wide if back else x
        return push(
            held, out.at[place, column, core], x_send.at[k, i], x_recv.at[k, i],
            frame=index(y, (x + i) % wide, core),
        )

    def across(k, back=False):
        place = (y + high - k) % high
        side = 1 - core if back else core
        held = out.at[place, :, side]
        return push(out.at[place, :, core], held, c_send.at[k], c_recv.at[k], frame=sibling)

    near = sorted(range(1, high), key=lambda k: min(k, high - k))
    for k in near:
        along_y(k).start()
    for i in range(1, wide):
        along_x(0, i).start()
    for k in near:
        along_y(k, True).wait_recv()
        for i in range(1, wide):
            along_x(k, i).start()
    own.wait()
    for k in [0, *near]:
        for i in range(1, wide):
            along_x(k, i, True).wait_recv()
        across(k).start()
    for k in [0, *near]:
        across(k, True).wait_recv()
    for k in near:
        along_y(k).wait_send()
    for k in [0, *near]:
        for i in range(1, wide):
            along_x(k, i).wait_send()
        across(k).wait_send()


def gather(chunk):
    count = lax.axis_size("frame")
    wide = PLANE_WIDE
    high = count // (2 * wide)
    out = pl.pallas_call(
        gather_kernel,
        out_shape=jax.ShapeDtypeStruct((high, wide, 2, *chunk.shape), chunk.dtype),
        in_specs=[VMEM],
        out_specs=VMEM,
        scratch_shapes=[
            pltpu.SemaphoreType.DMA((high,)),
            pltpu.SemaphoreType.DMA((high,)),
            pltpu.SemaphoreType.DMA((high, wide)),
            pltpu.SemaphoreType.DMA((high, wide)),
            pltpu.SemaphoreType.DMA((high,)),
            pltpu.SemaphoreType.DMA((high,)),
            pltpu.SemaphoreType.DMA,
        ],
        compiler_params=pltpu.CompilerParams(collective_id=0, has_side_effects=True),
        name="gather",
    )(chunk)
    return out.reshape(count, *chunk.shape)


def plane_copies(frame, count, pairs, send, recv):
    def out_piece(i, k):
        peer = (frame + k) % count
        src, dst = pairs[i]
        return push(src.at[peer], dst.at[frame], send.at[i, k], recv.at[i, k], frame=peer)

    def in_piece(i, k):
        origin = (frame + count - k) % count
        src, dst = pairs[i]
        return push(src.at[origin], dst.at[origin], send.at[i, k], recv.at[i, k], frame=origin)

    return out_piece, in_piece


def plane_start(frame, count, pairs, send, recv, own_sem, some=None):
    out_piece, unused = plane_copies(frame, count, pairs, send, recv)
    for i, (src, dst) in enumerate(pairs):
        pltpu.make_async_copy(src.at[frame], dst.at[frame], own_sem.at[i]).start()

    def begin(k):
        for i in range(len(pairs)):
            out_piece(i, k).start()

    each(1, count if some is None else some, begin)
    return begin


def plane_wait(frame, count, pairs, send, recv, own_sem):
    out_piece, in_piece = plane_copies(frame, count, pairs, send, recv)

    def end(k):
        for i in range(len(pairs)):
            in_piece(i, k).wait_recv()
            out_piece(i, k).wait_send()

    each(1, count, end)
    for i, (src, dst) in enumerate(pairs):
        pltpu.make_async_copy(src.at[frame], dst.at[frame], own_sem.at[i]).wait()


def exchange_chain_kernel(
    per_head, xs, gs, end_local, own_grad, decay, rx, rg, state_in, later, fwd_out, bwd_out, send, recv, own_sem,
    fwd_send, fwd_recv, bwd_send, bwd_recv,
):
    frame, row = lax.axis_index("frame"), lax.axis_index("row")
    count, bands = lax.axis_size("frame"), lax.axis_size("row")
    height = end_local.shape[0] // CHAIN_CHUNKS
    barrier = pltpu.get_barrier_semaphore()
    each(1, count, lambda k: tell(barrier, frame=(frame + k) % count))

    @pl.when(row > 0)
    def _():
        tell(barrier, row=row - 1)

    @pl.when(row < bands - 1)
    def _():
        tell(barrier, row=row + 1)

    neighbours = jnp.where(row > 0, 1, 0) + jnp.where(row < bands - 1, 1, 0)
    pl.semaphore_wait(barrier, count - 1 + neighbours)

    def rows_of(c):
        return pl.ds(pl.multiple_of(c * height, height), height)

    def fwd(c):
        where = rows_of(c)
        return push(fwd_out.at[where], state_in.at[where], fwd_send.at[c], fwd_recv.at[c], row=row + 1)

    def bwd(c):
        where = rows_of(c)
        return push(bwd_out.at[where], later.at[where], bwd_send.at[c], bwd_recv.at[c], row=row - 1)

    def fwd_in(c):
        where = rows_of(c)
        return push(fwd_out.at[where], state_in.at[where], fwd_send.at[c], fwd_recv.at[c], row=row - 1)

    def bwd_in(c):
        where = rows_of(c)
        return push(bwd_out.at[where], later.at[where], bwd_send.at[c], bwd_recv.at[c], row=row + 1)

    def join(c, before, own, result):
        for j in range(height // per_head):
            where = pl.ds(pl.multiple_of(c * height + j * per_head, per_head), per_head)
            factor = decay[0, c * (height // per_head) + j]
            result[where, :] = (
                before[where, :].astype(jnp.float32) * factor + own[where, :]
            ).astype(result.dtype)

    @pl.when(row == 0)
    def _():
        state_in[...] = jnp.zeros_like(state_in)
        for c in range(CHAIN_CHUNKS):
            fwd_out[rows_of(c), :] = end_local[rows_of(c), :].astype(fwd_out.dtype)
            fwd(c).start()

    @pl.when(row == bands - 1)
    def _():
        later[...] = jnp.zeros_like(later)
        for c in range(CHAIN_CHUNKS):
            bwd_out[rows_of(c), :] = own_grad[rows_of(c), :].astype(bwd_out.dtype)
            bwd(c).start()

    slots = CHAIN_CHUNKS + (bands - 1) * CHAIN_LAG
    ahead = 1 + PLANE_AHEAD
    per_slot = -(-(count - ahead) // (slots - PLANE_LATEST))
    begin = plane_start(frame, count, [(xs, rx), (gs, rg)], send, recv, own_sem, ahead)

    def slot(s):
        f = s - row * CHAIN_LAG
        b = s - (bands - 1 - row) * CHAIN_LAG

        @pl.when(jnp.logical_and(row > 0, jnp.logical_and(f >= 0, f < CHAIN_CHUNKS)))
        def _():
            fwd_in(f).wait_recv()

            @pl.when(row < bands - 1)
            def _():
                join(f, state_in, end_local, fwd_out)
                fwd(f).start()

        @pl.when(jnp.logical_and(row < bands - 1, jnp.logical_and(b >= 0, b < CHAIN_CHUNKS)))
        def _():
            bwd_in(b).wait_recv()

            @pl.when(row > 0)
            def _():
                join(b, later, own_grad, bwd_out)
                bwd(b).start()

        first = jnp.minimum(ahead + s * per_slot, count)
        each(first, jnp.minimum(first + per_slot, count), begin)

    each(0, slots, slot)
    plane_wait(frame, count, [(xs, rx), (gs, rg)], send, recv, own_sem)

    @pl.when(row < bands - 1)
    def _():
        for c in range(CHAIN_CHUNKS):
            fwd(c).wait_send()

    @pl.when(row > 0)
    def _():
        for c in range(CHAIN_CHUNKS):
            bwd(c).wait_send()


def exchange_chain(per_head, xs, gs, end_local, own_grad, decay):
    count = lax.axis_size("frame")
    state = jax.ShapeDtypeStruct(end_local.shape, jnp.bfloat16)
    return pl.pallas_call(
        functools.partial(exchange_chain_kernel, per_head),
        out_shape=(
            jax.ShapeDtypeStruct(xs.shape, xs.dtype),
            jax.ShapeDtypeStruct(gs.shape, gs.dtype),
            state,
            state,
        ),
        in_specs=[ANY, ANY, VMEM, VMEM, SMEM],
        out_specs=(ANY, ANY, VMEM, VMEM),
        scratch_shapes=[
            pltpu.VMEM(end_local.shape, jnp.bfloat16),
            pltpu.VMEM(end_local.shape, jnp.bfloat16),
            pltpu.SemaphoreType.DMA((2, count)),
            pltpu.SemaphoreType.DMA((2, count)),
            pltpu.SemaphoreType.DMA((2,)),
            pltpu.SemaphoreType.DMA((CHAIN_CHUNKS,)),
            pltpu.SemaphoreType.DMA((CHAIN_CHUNKS,)),
            pltpu.SemaphoreType.DMA((CHAIN_CHUNKS,)),
            pltpu.SemaphoreType.DMA((CHAIN_CHUNKS,)),
        ],
        compiler_params=pltpu.CompilerParams(collective_id=1, has_side_effects=True),
        name="exchange_chain",
    )(xs, gs, end_local, own_grad, decay)


def finish_kernel(
    ts, bs, wp, ws, mixed_part, pre_part, tokens, scale,
    mixed_out, tokens_out, mod_out, weight_out,
    rt, rb, proj_parts, step_parts, pre, band, band_low, core_part, half, half_low, y_parts, x_parts, total,
    mod_src, a_parts, b_src, b_parts, z_src, z_parts,
    c_send, c_recv, y_send, y_recv, x_send, x_recv, d_send, d_recv, d_own,
    a_send, a_recv, b_send, b_recv, z_send, z_recv, t_send, t_recv, t_own, w_send, w_recv, w_own,
):
    frame, row = lax.axis_index("frame"), lax.axis_index("row")
    bands = lax.axis_size("row")
    length, width = pre.shape
    lanes = mod_src.shape[2]
    blocks = width // lanes
    wide, high = x_parts.shape[0], y_parts.shape[0]
    tall = total.shape[0]
    core, x, y = frame % 2, frame // 2 % wide, frame // (2 * wide)
    side = half.shape[0]
    coef = proj_parts.shape[2]

    def index(y, x, core):
        return (y * wide + x) * 2 + core

    sibling = index(y, x, 1 - core)
    per_home = 2
    home = row * high + core * (high // 2) + y // per_home
    piece = y % per_home
    from_row, from_core, from_x = frame // high, frame % high // (high // 2), row // per_home

    def source(i):
        return index(frame % (high // 2) * per_home + i, from_x, from_core)

    def other(f, r):
        return jnp.logical_or(f != frame, r != row)

    group = 2 * wide
    own = x * 2 + core

    def mate(k):
        return y * group + (own + k) % group

    barrier = pltpu.get_barrier_semaphore()
    count = lax.axis_size("frame")
    each(1, count, lambda k: tell(barrier, frame=(frame + k) % count))
    each(1, bands, lambda k: tell(barrier, row=(row + k) % bands))
    for i in range(per_home):

        @pl.when(other(source(i), from_row))
        def _():
            tell(barrier, frame=source(i), row=from_row)

    local = jnp.where(home == frame, jnp.where(row // per_home == x, 1, 0), 0)

    squares = jnp.zeros((length, lanes), jnp.float32)
    for j in range(blocks):
        where = slice(j * lanes, (j + 1) * lanes)
        squares += tokens[:, where].astype(jnp.float32) ** 2
    inverse = lax.rsqrt(jnp.sum(squares, axis=1, keepdims=True) * (1.0 / width) + norm_eps)
    pl.semaphore_wait(barrier, count - 1 + bands - 1 + per_home - local)

    def rows_at(k, size):
        return pl.ds(pl.multiple_of(k * size, size), size)

    share = band.shape[0]

    def pieces(j):
        return (wp.at[rows_at(j, share), :], proj_parts), (ws.at[:, rows_at(j, share)], step_parts)

    def w_out(i, k):
        peer = (row + k) % bands
        src, dst = pieces(peer)[i]
        return push(src, dst.at[row], w_send.at[i, k], w_recv.at[i, k], row=peer)

    def w_in(i, k):
        origin = (row + bands - k) % bands
        src, dst = pieces(origin)[i]
        return push(src, dst.at[origin], w_send.at[i, k], w_recv.at[i, k], row=origin)

    def w_self(i):
        src, dst = pieces(row)[i]
        return pltpu.make_async_copy(src, dst.at[row], w_own.at[i])

    def w_begin(k):
        for i in range(2):
            w_out(i, k).start()

    def w_end(k):
        for i in range(2):
            w_in(i, k).wait_recv()
            w_out(i, k).wait_send()

    for i in range(2):
        w_self(i).start()
    each(1, bands, w_begin)
    plane_start(frame, count, [(bs, rb), (ts, rt)], t_send, t_recv, t_own)
    each(1, bands, w_end)
    for i in range(2):
        w_self(i).wait()

    step = 2 * tall
    for i in range(band.shape[0] // step):
        rows = slice(i * step, (i + 1) * step)
        part = proj_parts[0, rows, :].astype(jnp.float32)
        for j in range(1, proj_parts.shape[0]):
            part += proj_parts[j, rows, :].astype(jnp.float32)
        band[rows, :coef] = part
    part = step_parts[0].astype(jnp.float32)
    for j in range(1, step_parts.shape[0]):
        part += step_parts[j].astype(jnp.float32)
    filled = jnp.concatenate([part, jnp.zeros((lanes - part.shape[0], part.shape[1]), jnp.float32)], axis=0)
    band[:, coef:] = filled.T
    band_low[...] = band[...].astype(band_low.dtype)
    across = push(band_low.at[rows_at(1 - core, side), :], core_part, c_send, c_recv, frame=sibling)
    across.start()

    across.wait_recv()
    half[...] = band[rows_at(core, side), :] + core_part[...].astype(jnp.float32)
    half_low[...] = half[...].astype(half_low.dtype)

    def y_out(k):
        peer = (y + k) % high
        return push(
            half_low.at[rows_at(peer, tall), :], y_parts.at[y], y_send.at[k], y_recv.at[k],
            frame=index(peer, x, core),
        )

    def y_in(k):
        origin = (y + high - k) % high
        return push(
            half_low.at[rows_at(0, tall), :], y_parts.at[origin], y_send.at[k], y_recv.at[k],
            frame=index(origin, x, core),
        )

    for k in range(1, high):
        y_out(k).start()
    y_parts[pl.ds(y, 1)] = half_low[rows_at(y, tall), :][None]

    plane_wait(frame, count, [(bs, rb), (ts, rt)], t_send, t_recv, t_own)

    along = jnp.zeros((length, lanes), jnp.float32)
    for j in range(blocks):
        where = slice(j * lanes, (j + 1) * lanes)
        value = pre_part[:, where] + read(rb, where).astype(jnp.float32)
        pre[:, where] = value
        matched = value * (tokens[:, where].astype(jnp.float32) * inverse)
        to_y, to_x = j // wide, j % wide
        mod_src[to_x, to_y : to_y + 1, :] = jnp.sum(value, axis=0, keepdims=True)
        to_y += blocks // wide
        mod_src[to_x, to_y : to_y + 1, :] = jnp.sum(matched, axis=0, keepdims=True)
        along += matched * (1.0 + scale[:, where])

    def a_out(k):
        peer = (own + k) % group
        return push(mod_src.at[peer // 2], a_parts.at[own], a_send.at[k], a_recv.at[k], frame=mate(k))

    def a_in(k):
        origin = (own + group - k) % group
        return push(mod_src.at[0], a_parts.at[origin], a_send.at[k], a_recv.at[k], frame=mate(k))

    for k in range(1, group):
        a_out(k).start()
    a_parts[pl.ds(own, 1)] = mod_src[pl.ds(x, 1)]
    for k in range(1, high):
        y_in(k).wait_recv()
    x_parts[pl.ds(x, 1)] = jnp.sum(y_parts[...].astype(jnp.float32), axis=0)[None]

    def x_out(k):
        return push(
            x_parts.at[x], x_parts.at[x], x_send.at[k], x_recv.at[k], frame=index(y, (x + k) % wide, core)
        )

    def x_in(k):
        origin = (x + wide - k) % wide
        return push(
            x_parts.at[origin], x_parts.at[origin], x_send.at[k], x_recv.at[k], frame=index(y, origin, core)
        )

    for k in range(1, wide):
        x_out(k).start()
    along = jnp.sum(along, axis=1, keepdims=True) * (1.0 / width)
    for j in range(blocks):
        where = slice(j * lanes, (j + 1) * lanes)
        unit = tokens[:, where].astype(jnp.float32) * inverse
        pulled = pre[:, where] * (1.0 + scale[:, where])
        tokens_out[:, where] = (inverse * (pulled - unit * along)).astype(tokens_out.dtype)
        mixed_out[:, where] = (mixed_part[:, where] + read(rt, where).astype(jnp.float32)).astype(
            mixed_out.dtype
        )

    for k in range(1, group):
        a_in(k).wait_recv()
    b_src[...] = jnp.sum(a_parts[...], axis=0)

    def b_out(k):
        return push(
            b_src, b_parts.at[y], b_send.at[k], b_recv.at[k], frame=index((y + k) % high, x, core)
        )

    def b_in(k):
        origin = (y + high - k) % high
        return push(b_src, b_parts.at[origin], b_send.at[k], b_recv.at[k], frame=index(origin, x, core))

    for k in range(1, high):
        b_out(k).start()
    b_parts[pl.ds(y, 1)] = b_src[...][None]
    for k in range(1, wide):
        x_in(k).wait_recv()
    total[...] = jnp.sum(x_parts[...], axis=0)

    def d_out(i):
        return push(total, weight_out.at[piece], d_send.at[i], d_recv.at[piece], frame=home, row=x * per_home + i)

    def d_in(i):
        return push(total, weight_out.at[i], d_send.at[0], d_recv.at[i], frame=source(i), row=from_row)

    d_self = pltpu.make_async_copy(total, weight_out.at[piece], d_own)
    for i in range(per_home):
        away = other(home, x * per_home + i)

        @pl.when(away)
        def _():
            d_out(i).start()

        @pl.when(jnp.logical_not(away))
        def _():
            d_self.start()

    for k in range(1, high):
        b_in(k).wait_recv()
    z_src[...] = jnp.zeros_like(z_src)
    per_clip = high // CLIPS
    for c in range(CLIPS):
        chosen = b_parts[c * per_clip, pl.ds(y, 1), :]
        for i in range(1, per_clip):
            chosen += b_parts[c * per_clip + i, pl.ds(y, 1), :]
        z_src[c : c + 1, :] = chosen

    def z_out(k):
        return push(z_src, z_parts.at[row], z_send.at[k], z_recv.at[k], row=(row + k) % bands)

    def z_in(k):
        origin = (row + bands - k) % bands
        return push(z_src, z_parts.at[origin], z_send.at[k], z_recv.at[k], row=origin)

    for k in range(1, z_parts.shape[0]):
        z_out(k).start()
    z_parts[pl.ds(row, 1)] = z_src[...][None]
    for k in range(1, z_parts.shape[0]):
        z_in(k).wait_recv()
    mod_out[...] = jnp.sum(z_parts[...], axis=0)
    for i in range(per_home):
        came = other(source(i), from_row)

        @pl.when(came)
        def _():
            d_in(i).wait_recv()

        @pl.when(jnp.logical_not(came))
        def _():
            d_self.wait()

    across.wait_send()
    for k in range(1, group):
        a_out(k).wait_send()
    for k in range(1, high):
        y_out(k).wait_send()
        b_out(k).wait_send()
    for k in range(1, wide):
        x_out(k).wait_send()
    for k in range(1, z_parts.shape[0]):
        z_out(k).wait_send()
    for i in range(per_home):

        @pl.when(other(home, x * per_home + i))
        def _():
            d_out(i).wait_send()


def finish(ts, bs, wp, ws, mixed_part, pre_part, tokens, scale):
    count, bands = lax.axis_size("frame"), lax.axis_size("row")
    length, width = tokens.shape
    lanes = 128
    wide = PLANE_WIDE
    high = count // (2 * wide)
    share, coef = width // bands, wp.shape[1] + lanes
    tall = share // 2 // high
    low = jax.ShapeDtypeStruct(tokens.shape, tokens.dtype)
    f32, bf16 = jnp.float32, jnp.bfloat16
    sems = pltpu.SemaphoreType.DMA
    return pl.pallas_call(
        finish_kernel,
        out_shape=(
            low,
            low,
            jax.ShapeDtypeStruct((8, lanes), f32),
            jax.ShapeDtypeStruct((2, tall, coef), f32),
        ),
        in_specs=[VMEM] * 8,
        out_specs=(VMEM,) * 4,
        scratch_shapes=[
            pltpu.VMEM(ts.shape, bf16),
            pltpu.VMEM(bs.shape, bf16),
            pltpu.VMEM((bands, share, wp.shape[1]), bf16),
            pltpu.VMEM((bands, ws.shape[0], share), bf16),
            pltpu.VMEM((length, width), f32),
            pltpu.VMEM((share, coef), f32),
            pltpu.VMEM((share, coef), bf16),
            pltpu.VMEM((share // 2, coef), bf16),
            pltpu.VMEM((share // 2, coef), f32),
            pltpu.VMEM((share // 2, coef), bf16),
            pltpu.VMEM((high, tall, coef), bf16),
            pltpu.VMEM((wide, tall, coef), f32),
            pltpu.VMEM((tall, coef), f32),
            pltpu.VMEM((wide, high, lanes), f32),
            pltpu.VMEM((2 * wide, high, lanes), f32),
            pltpu.VMEM((high, lanes), f32),
            pltpu.VMEM((high, high, lanes), f32),
            pltpu.VMEM((8, lanes), f32),
            pltpu.VMEM((bands, 8, lanes), f32),
            sems,
            sems,
            sems((high,)),
            sems((high,)),
            sems((wide,)),
            sems((wide,)),
            sems((2,)),
            sems((2,)),
            sems,
            sems((2 * wide,)),
            sems((2 * wide,)),
            sems((high,)),
            sems((high,)),
            sems((bands,)),
            sems((bands,)),
            sems((2, count)),
            sems((2, count)),
            sems((2,)),
            sems((2, bands)),
            sems((2, bands)),
            sems((2,)),
        ],
        compiler_params=pltpu.CompilerParams(collective_id=3, has_side_effects=True, vmem_limit_bytes=BIG),
        name="finish",
    )(ts, bs, wp, ws, mixed_part, pre_part, tokens, scale)


def time_embed(timestep, embed_dim):
    half_dim = embed_dim // 2
    frequency = jnp.exp(-math.log(10000.0) * jnp.arange(half_dim, dtype=jnp.float32) / half_dim)
    angles = timestep.astype(jnp.float32)[:, None] * frequency[None, :]
    return jax.nn.silu(jnp.concatenate([jnp.cos(angles), jnp.sin(angles)], axis=1))


def halves(values):
    high = values.astype(jnp.bfloat16)
    return high, (values - high.astype(jnp.float32)).astype(jnp.bfloat16)


def mm(a, b):
    return jnp.dot(a, b, preferred_element_type=jnp.float32)


def mm_nt(a, b):
    return lax.dot_general(a, b, (((1,), (1,)), ((), ())), preferred_element_type=jnp.float32)


def mm_tn(a, b):
    return lax.dot_general(a, b, (((0,), (0,)), ((), ())), preferred_element_type=jnp.float32)


def with_ones(ones, values, dot):
    first = values.astype(jnp.bfloat16)
    rest = values - first.astype(jnp.float32)
    second = rest.astype(jnp.bfloat16)
    third = (rest - second.astype(jnp.float32)).astype(jnp.bfloat16)
    return dot(ones, first) + dot(ones, second) + dot(ones, third)


def earlier_mask(length, sites):
    t = lax.broadcasted_iota(jnp.int32, (length, length), 0)
    u = lax.broadcasted_iota(jnp.int32, (length, length), 1)
    return jnp.logical_and(u <= t, lax.rem(t, sites) == lax.rem(u, sites))


def steps_of(logits, bias, rate, mask):
    raised = logits.astype(jnp.float32) + bias
    step = jnp.maximum(raised, 0.0) + jnp.log1p(jnp.exp(-jnp.abs(raised)))
    lower = jnp.where(mask, 1.0, 0.0).astype(jnp.bfloat16)
    return raised, step, with_ones(lower, -step * rate, mm)


def stacked(values):
    parts = [halves(v) for v in values]
    return jnp.concatenate([p[0] for p in parts] + [p[1] for p in parts], axis=0)


def split_sum(product, sizes):
    total = sum(sizes)
    result, start = [], 0
    for size in sizes:
        result.append(product[start : start + size] + product[total + start : total + start + size])
        start += size
    return result


def spread(columns, expand, where):
    length = columns.shape[0]
    return split_sum(mm(columns, expand[:, where]), [length // 2])[0]


def per_head(values, expand, where):
    return split_sum(mm_nt(stacked(values), expand[:, where]), [v.shape[0] for v in values])


def head_kernel(
    tokens, grad, weights, step_w, shift, scale, small, expand,
    normed_out, coeff_out, logit_out, end_out, own_out, decay_out,
):
    length, width = tokens.shape
    lanes = step_w.shape[1]
    values = tokens[...].astype(jnp.float32)
    inverse = lax.rsqrt(jnp.mean(values * values, axis=1, keepdims=True) + norm_eps)
    normed_out[...] = (values * inverse * (1.0 + scale[...]) + shift[...]).astype(jnp.bfloat16)
    project(normed_out, weights, step_w, coeff_out, logit_out)
    b_part, c_part = coeff_out[:, :lanes], coeff_out[:, lanes:]
    mask = earlier_mask(length, 1)
    unused, step, log = steps_of(logit_out[...], small[0:1, :], small[1:2, :], mask)
    last = log[length - 1 :, :]
    decay_out[...] = jnp.exp(last)
    lead = jnp.exp(last - log) * step
    reach = jnp.exp(log) * (1.0 / lanes)
    columns = stacked([lead, reach])
    for j in range(width // lanes):
        where = slice(j * lanes, (j + 1) * lanes)
        wide = spread(columns, expand, where)
        scaled = (normed_out[:, where].astype(jnp.float32) * wide[:length]).astype(jnp.bfloat16)
        end_out[where, :] = mm_tn(scaled, b_part)
        pulled = (grad[:, where].astype(jnp.float32) * wide[length:]).astype(jnp.bfloat16)
        own_out[where, :] = mm_tn(pulled, c_part)


def project(normed, weights, step_w, coeff_out, logit_out):
    lanes = step_w.shape[1]
    count = weights.shape[0]
    depth = normed.shape[1] // count
    for i in range(2):
        w = weights[:, i * depth : (i + 1) * depth, :].reshape(count * depth, lanes)
        coeff_out[:, i * lanes : (i + 1) * lanes] = mm(normed[...], w).astype(jnp.bfloat16)
    logit_out[...] = mm(normed[...], step_w[...]).astype(jnp.bfloat16)


def read(ref, where):
    if len(ref.shape) == 2:
        return ref[:, where]
    values = ref[:, :, where]
    return values.reshape(ref.shape[0] * ref.shape[1], values.shape[2])


def write(ref, where, values):
    values = values.astype(ref.dtype)
    if len(ref.shape) == 2:
        ref[:, where] = values
    else:
        ref[:, :, where] = values.reshape(*ref.shape[:2], values.shape[1])


def scan_pass(
    x_ref, g_ref, coeffs, logits, bias, rate, weights, step_w, expand, skip, state, later,
    mixed_ref, dx_ref, back_ref, wp_ref, ws_ref, sites, first,
):
    length, width = x_ref.shape
    lanes = coeffs.shape[1] // 2
    space = state is not None
    b_part, c_part = coeffs[:, :lanes], coeffs[:, lanes:]
    mask = earlier_mask(length, sites)
    raised, step, log = steps_of(logits[...], bias, rate, mask)
    log_t = log.T
    scores = jnp.where(mask, mm_nt(c_part, b_part) * (1.0 / lanes), 0.0)
    left = lax.broadcasted_iota(jnp.int32, (length, lanes), 1) < lanes // 2
    d_scores = jnp.zeros((length, length), jnp.float32)
    pull_out = jnp.zeros((length, lanes), jnp.float32)
    pull_in = jnp.zeros((length, lanes), jnp.float32)
    d_b = jnp.zeros((length, lanes), jnp.float32)
    d_c = jnp.zeros((length, lanes), jnp.float32)
    if space:
        last = log[length - 1 :, :]
        reach_all = jnp.exp(log) * (1.0 / lanes)
        fade_all = jnp.exp(last - log)
        d_last = jnp.zeros((16, lanes), jnp.float32)
        state_rows = []
        columns = stacked([step, reach_all, fade_all, skip])
    else:
        columns = stacked([step])
    for j in range(width // lanes):
        where = slice(j * lanes, (j + 1) * lanes)
        x, g = read(x_ref, where), read(g_ref, where)
        wide_x, wide_g = x.astype(jnp.float32), g.astype(jnp.float32)
        spread_all = spread(columns, expand, where)
        step_x = spread_all[:length]
        stepped_wide = wide_x * step_x
        stepped = stepped_wide.astype(jnp.bfloat16)
        falls = []
        for h in (2 * j, 2 * j + 1):
            falls.append(jnp.exp(jnp.minimum(log[:, h : h + 1] - log_t[h : h + 1, :], 0.0)))
        pair = [(scores * fall).astype(jnp.bfloat16) for fall in falls]
        outs = mm(jnp.concatenate(pair, axis=0), stepped)
        backs = mm_tn(jnp.concatenate(pair, axis=1), g)
        left_g = jnp.where(left, wide_g, 0.0).astype(jnp.bfloat16)
        right_g = jnp.where(left, 0.0, wide_g).astype(jnp.bfloat16)
        d_pair = mm_nt(jnp.concatenate([left_g, right_g], axis=0), stepped)
        d_scores += d_pair[:length] * falls[0] + d_pair[length:] * falls[1]
        out = jnp.where(left, outs[:length], outs[length:])
        d_step_x = jnp.where(left, backs[:length], backs[length:])
        if space:
            held, late = state[where, :], later[where, :]
            reach, fade = spread_all[length : 2 * length], spread_all[2 * length : 3 * length]
            gain = spread_all[3 * length : 3 * length + 1]
            out += mm_nt(c_part, held) * reach
            d_c += mm((wide_g * reach).astype(jnp.bfloat16), held)
            from_end = mm_nt(b_part, late) * fade
            d_step_x += from_end
            d_b += mm((stepped_wide * fade).astype(jnp.bfloat16), late)
            to_last = jnp.sum(stepped_wide * from_end, axis=0, keepdims=True)
            both = held.astype(jnp.float32) * late.astype(jnp.float32)
            half = lanes // 2
            state_rows += [
                jnp.sum(both[:half], axis=0, keepdims=True),
                jnp.sum(both[half:], axis=0, keepdims=True),
            ]
            mixed_ref[:, where] = out + gain * wide_x
            direct = (wide_g * gain).astype(jnp.bfloat16).astype(jnp.float32)
            dx_ref[:, where] = step_x * d_step_x + direct
        else:
            write(mixed_ref, where, out)
            dx_ref[:, where] = step_x * d_step_x
        sums = [wide_g * out, wide_x * d_step_x]
        if space:
            sums.append(jnp.broadcast_to(to_last, (16, lanes)))
        sums = per_head(sums, expand, where)
        pull_out += sums[0]
        pull_in += sums[1]
        if space:
            d_last += sums[2]
    d_low = (jnp.where(mask, d_scores, 0.0) * (1.0 / lanes)).astype(jnp.bfloat16)
    d_c += mm(d_low, b_part)
    d_b += mm_tn(d_low, c_part)
    d_log = pull_out - step * pull_in
    if space:
        states = jnp.concatenate([*state_rows, jnp.zeros((lanes - len(state_rows), lanes), jnp.float32)], axis=0)
        high, low = halves(states)
        ones = jnp.ones((16, lanes), jnp.bfloat16)
        d_last += (mm_nt(ones, high) + mm_nt(ones, low)) * jnp.exp(last)
        at_end = lax.broadcasted_iota(jnp.int32, (length, lanes), 0) == length - 1
        d_log += jnp.where(at_end, d_last[:1, :], 0.0)
    lower = jnp.where(mask, 1.0, 0.0).astype(jnp.bfloat16)
    d_fall = with_ones(lower, d_log, mm_tn)
    d_step = pull_in - rate * d_fall
    d_logit = (d_step * jax.nn.sigmoid(raised)).astype(jnp.bfloat16)
    low_b, low_c = d_b.astype(jnp.bfloat16), d_c.astype(jnp.bfloat16)
    count = weights.shape[0]
    depth = width // count
    block = 8
    for k in range(count // block):
        cols = slice(k * block * depth, (k + 1) * block * depth)
        w_b = weights[k * block : (k + 1) * block, :depth, :].reshape(block * depth, lanes)
        w_c = weights[k * block : (k + 1) * block, depth : 2 * depth, :].reshape(block * depth, lanes)
        total = (
            dx_ref[:, cols] + mm_nt(low_b, w_b) + mm_nt(low_c, w_c) + mm_nt(d_logit, step_w[cols, :])
        )
        write(back_ref, cols, total)
        x = x_ref[:, cols]
        terms = ((wp_ref, cols, slice(0, lanes), mm_tn(x, low_b)), (wp_ref, cols, slice(lanes, None), mm_tn(x, low_c)))
        terms += ((ws_ref, slice(None), cols, mm_tn(d_logit, x)[: ws_ref.shape[0]]),)
        for ref, rows, columns, term in terms:
            ref[rows, columns] = term if first else ref[rows, columns] + term


def core_kernel(
    normed, grad, coeffs, logits, state, later, site_tokens, site_grad, weights, step_w, shift_all, scale_all,
    small, expand,
    mixed_out, pre_out, time_out, back_out, wp_out, ws_out, site_normed, site_coeffs, site_logits, dx, wp, ws,
):
    length, width = normed.shape
    bias, rate_space, rate_time = (small[i : i + 1, :] for i in range(3))
    skip = jnp.broadcast_to(small[3:4, :], (16, small.shape[1]))
    clips = shift_all.shape[0]
    sites = length // weights.shape[0]
    part = length // clips
    for c in range(clips):
        rows = slice(c * part, (c + 1) * part)
        frames = slice(c * part // sites, (c + 1) * part // sites)
        values = site_tokens[frames].reshape(part, width).astype(jnp.float32)
        inverse = lax.rsqrt(jnp.mean(values * values, axis=1, keepdims=True) + norm_eps)
        site_normed[rows, :] = (
            values * inverse * (1.0 + scale_all[c : c + 1, :]) + shift_all[c : c + 1, :]
        ).astype(jnp.bfloat16)
    project(site_normed, weights, step_w, site_coeffs, site_logits)
    scan_pass(
        site_normed, site_grad, site_coeffs, site_logits, bias, rate_time, weights, step_w, expand,
        None, None, None, time_out, dx, back_out, wp, ws, sites, True,
    )
    scan_pass(
        normed, grad, coeffs, logits, bias, rate_space, weights, step_w, expand,
        skip, state, later, mixed_out, dx, pre_out, wp, ws, 1, False,
    )
    wp_out[...] = wp[...].astype(jnp.bfloat16)
    ws_out[...] = ws[...].astype(jnp.bfloat16)


def head(tokens, grad, weights, step_w, shift, scale, small, expand):
    length, width = tokens.shape
    lanes = step_w.shape[1]
    low = functools.partial(jax.ShapeDtypeStruct, dtype=jnp.bfloat16)
    wide = functools.partial(jax.ShapeDtypeStruct, dtype=jnp.float32)
    return pl.pallas_call(
        head_kernel,
        out_shape=(
            low((length, width)),
            low((length, 2 * lanes)),
            low((length, lanes)),
            wide((width, lanes)),
            wide((width, lanes)),
            wide((1, lanes)),
        ),
        in_specs=[VMEM] * 8,
        out_specs=(VMEM,) * 6,
        compiler_params=pltpu.CompilerParams(vmem_limit_bytes=BIG),
        name="head",
    )(tokens, grad, weights, step_w, shift, scale, small, expand)


def core(heads, *operands):
    normed, coeffs, weights = operands[0], operands[2], operands[8]
    length, width = normed.shape
    lanes = coeffs.shape[1] // 2
    low = functools.partial(jax.ShapeDtypeStruct, dtype=jnp.bfloat16)
    wide = functools.partial(jax.ShapeDtypeStruct, dtype=jnp.float32)
    return pl.pallas_call(
        core_kernel,
        out_shape=(
            wide((length, width)),
            wide((length, width)),
            low(operands[6].shape),
            low(operands[6].shape),
            low((width, 2 * lanes)),
            low((heads, width)),
        ),
        in_specs=[VMEM] * 14,
        out_specs=(VMEM,) * 6,
        scratch_shapes=[
            pltpu.VMEM((length, width), jnp.bfloat16),
            pltpu.VMEM((length, 2 * lanes), jnp.bfloat16),
            pltpu.VMEM((length, lanes), jnp.bfloat16),
            pltpu.VMEM((length, width), jnp.float32),
            pltpu.VMEM((width, 2 * lanes), jnp.float32),
            pltpu.VMEM((heads, width), jnp.float32),
        ],
        compiler_params=pltpu.CompilerParams(vmem_limit_bytes=BIG),
        name="core",
    )(*operands)


def three_parts(values):
    first = lax.reduce_precision(values, 8, 7)
    second = lax.reduce_precision(values - first, 8, 7)
    return first, second, values - first - second


def per_device(
    tokens,
    cotangent,
    timestep,
    mod_weight,
    proj_weight,
    step_weight,
    step_bias,
    rate_space,
    rate_time,
    skip_gain,
):
    frame_count = lax.axis_size("frame")
    row_count = lax.axis_size("row")
    frame_id = lax.axis_index("frame")
    feat_width = tokens.shape[-1]
    band_len = tokens.shape[1] * tokens.shape[2]
    clip_count = timestep.shape[0]
    clip_frames = frame_count // clip_count
    site_count = band_len // frame_count
    head_count = rate_space.shape[0]
    state_size = proj_weight.shape[1] // 2
    depth = proj_weight.shape[0]
    clip_id = frame_id // clip_frames
    factor = (frame_count * row_count * band_len) ** (-0.5)
    tokens = tokens.reshape(band_len, feat_width)
    flat_grad = cotangent.reshape(band_len, feat_width)

    activated = time_embed(timestep, mod_weight.shape[0]).astype(jnp.bfloat16)
    mod_cols = jnp.dot(activated, mod_weight, preferred_element_type=jnp.float32)
    lane = state_size
    mod_rows = [part.reshape(-1, lane).astype(jnp.bfloat16) for part in three_parts(mod_cols)]
    rows = [proj_weight[:, :state_size], proj_weight[:, state_size:], step_weight.reshape(-1, lane), *mod_rows]
    used = sum(r.shape[0] for r in rows)
    chunk = jnp.concatenate([*rows, jnp.zeros((-used % 16, lane), jnp.bfloat16)], axis=0)
    gathered = gather(chunk)
    step_rows = depth * head_count // lane
    step_full = gathered[:, 2 * depth : 2 * depth + step_rows].reshape(feat_width, head_count)
    step_w = jnp.pad(step_full, ((0, 0), (0, lane - head_count)))
    mod_height = mod_rows[0].shape[0]
    mod_parts = gathered[:, 2 * depth + step_rows : 2 * depth + step_rows + 3 * mod_height]
    mod_parts = mod_parts.astype(jnp.float32).reshape(frame_count, 3, clip_count, -1)
    modulation = mod_parts[:, 0] + mod_parts[:, 1] + mod_parts[:, 2]
    modulation = modulation.transpose(1, 0, 2).reshape(clip_count, 2 * feat_width)
    shift_all, scale_all = modulation[:, :feat_width], modulation[:, feat_width:]
    shift_vec = lax.dynamic_index_in_dim(shift_all, clip_id, 0)
    scale_vec = lax.dynamic_index_in_dim(scale_all, clip_id, 0)

    small = jnp.pad(jnp.stack([step_bias, rate_space, rate_time, skip_gain]), ((0, 4), (0, lane - head_count)))
    channel_head = jnp.arange(feat_width) // (feat_width // head_count)
    expand = (channel_head[None, :] == jnp.arange(lane)[:, None]).astype(jnp.bfloat16)
    normed, coeffs, logits, end_local, own_grad, end_decay = head(
        tokens, flat_grad, gathered, step_w, shift_vec, scale_vec, small, expand
    )
    site_tokens, site_grad, state_in, later_grad = exchange_chain(
        feat_width // head_count,
        tokens.reshape(frame_count, site_count, feat_width),
        flat_grad.reshape(frame_count, site_count, feat_width),
        end_local,
        own_grad,
        end_decay,
    )
    mixed_part, pre_part, time_out, time_back, proj_grad, step_grad = core(
        head_count,
        normed,
        flat_grad,
        coeffs,
        logits,
        state_in,
        later_grad,
        site_tokens,
        site_grad,
        gathered,
        step_w,
        shift_all,
        scale_all,
        small,
        expand,
    )
    mixed, d_tokens, mod_sum, weight_sum = finish(
        time_out,
        time_back,
        proj_grad,
        step_grad,
        mixed_part,
        pre_part,
        tokens,
        scale_vec,
    )
    weight_rows = weight_sum.reshape(depth, -1) * factor
    grad_proj = weight_rows[:, : 2 * state_size]
    grad_step = weight_rows[:, 2 * state_size : 2 * state_size + head_count]
    mod_width = mod_weight.shape[1]
    mod_half = lax.dynamic_slice_in_dim(mod_sum[:clip_count], frame_id % 2 * mod_width, mod_width, axis=1)
    grad_mod = (
        jnp.dot(activated.astype(jnp.float32).T, mod_half, precision=lax.Precision.HIGHEST) * factor
    )
    shape = cotangent.shape
    return (
        mixed.reshape(shape),
        d_tokens.reshape(shape),
        grad_proj,
        grad_step,
        grad_mod,
    )


def solution(mesh):
    placed = (
        P("frame", "row", None, None),
        P("frame", "row", None, None),
        P(),
        P(None, "frame"),
        P("frame", None),
        P("frame", None),
        P(),
        P(),
        P(),
        P(),
    )
    return jax.shard_map(
        per_device,
        mesh=mesh,
        in_specs=placed,
        out_specs=(
            P("frame", "row", None, None),
            P("frame", "row", None, None),
            P("frame", None),
            P("frame", None),
            P(None, "frame"),
        ),
        check_vma=False,
    )
```
